256 devices in a mesh: ha: 4 (over z_hi), wa: 8 (over z_lo, x), hd: 8 (over y, core).
Axes of the slice: x: 4, y: 4, z: 8 (z_hi: 4, z_lo: 2; z = z_hi * 2 + z_lo), core: 2. Of those that a mesh axis runs over, the one named last changes fastest.
Arguments:
- query_in: bfloat16 [4, 8, 256, 3072], P('ha', 'wa', 'hd'), may hold values from -6 to 6
- key_in: bfloat16 [4, 8, 256, 3072], P('ha', 'wa', 'hd'), may hold values from -6 to 6
- value_in: bfloat16 [4, 8, 256, 3072], P('ha', 'wa', 'hd'), may hold values from -6 to 6
- out_fwd: bfloat16 [4, 8, 256, 3072], P('ha', 'wa', 'hd'), may hold values from -6 to 6
- grad_out: bfloat16 [4, 8, 256, 3072], P('ha', 'wa', 'hd'), may hold values from -6 to 6
- log_norm: float32 [4, 8, 256, 24], P('ha', 'wa', 'hd'), may hold values from 4 to 6
Outputs:
- grad_query: bfloat16 [4, 8, 256, 3072], P('ha', 'wa', 'hd')
- grad_key: bfloat16 [4, 8, 256, 3072], P('ha', 'wa', 'hd')
- grad_value: bfloat16 [4, 8, 256, 3072], P('ha', 'wa', 'hd')
The draws below stay inside these ranges and needn't reach their ends.
All inputs are finite; a program needn't handle non-finite values.
Results may differ from the reference program's by a relative error of at most 0.009.
Values may be sent and summed in bfloat16 or wider, within the bound.
A program may use at most 64 MiB of HBM per device.

```python
import jax
import jax.numpy as jnp
from jax import lax

HEADS = 24
HD = 128
TILE = 256
NTH = 4
NTW = 8
CHAN = 3072


def block_scale(stream_key, shape, cuts, least, largest):
    factor_of, own = 1.0, jax.random.fold_in(stream_key, 6)
    for axis_at, parts in cuts:
        heights = jnp.exp(jax.random.uniform(jax.random.fold_in(own, axis_at), (parts,), jnp.float32, least / len(cuts), largest / len(cuts)))
        factor_of = factor_of * jnp.repeat(heights, shape[axis_at] // parts).reshape([-1 if axis == axis_at else 1 for axis in range(len(shape))])
    return factor_of


def centred(rng, dims, spread, bound, pieces=(), kind=jnp.bfloat16):
    gain = block_scale(rng, dims, pieces, -0.22, 0.18) if pieces else 1.0
    drawn = jax.random.normal(rng, dims, jnp.float32) * spread * gain
    return jnp.minimum(jnp.maximum(drawn, -bound), bound).astype(kind)


def setup_inputs(seed: int = 0) -> dict:
    streams_of = jax.random.split(jax.random.key(seed), 7)
    query_in = centred(streams_of[0], (NTH, NTW, TILE, CHAN), 1.0, 6.0, ((0, 4), (1, 8), (2, 8)))
    key_in = centred(streams_of[1], (NTH, NTW, TILE, CHAN), 1.0, 6.0, ((0, 4), (1, 8), (2, 8)))
    value_in = centred(streams_of[2], (NTH, NTW, TILE, CHAN), 1.0, 6.0, ((0, 4), (1, 8), (2, 8)))
    out_fwd = centred(streams_of[3], (NTH, NTW, TILE, CHAN), 1.0, 6.0, ((0, 4), (1, 8), (2, 8)))
    grad_out = centred(streams_of[4], (NTH, NTW, TILE, CHAN), 1.0, 6.0, ((0, 4), (1, 8), (2, 8)))
    log_norm = jnp.clip(4.0 + 2.0 * jax.random.uniform(streams_of[5], (NTH, NTW, TILE, HEADS), jnp.float32) ** block_scale(streams_of[5], (NTH, NTW, TILE, HEADS), ((0, 4), (1, 8), (2, 8)), -0.2, 0.2), 4.0, 6.0)
    return dict(query_in=query_in, key_in=key_in, value_in=value_in, out_fwd=out_fwd, grad_out=grad_out, log_norm=log_norm)


def one_head(operands):
    query_h, key_h, value_h, grad_h, norm_h, dots_h = operands
    rows_h, rows_w = query_h.shape[0], query_h.shape[1]
    softmax_scale = HD ** -0.5
    pad_spec = ((1, 1), (1, 1), (0, 0), (0, 0))
    key_pad = jnp.pad(key_h.astype(jnp.float32), pad_spec)
    value_pad = jnp.pad(value_h.astype(jnp.float32), pad_spec)
    query_f = query_h.astype(jnp.float32)
    grad_f = grad_h.astype(jnp.float32)
    grad_q = jnp.zeros(query_h.shape, jnp.float32)
    key_acc = jnp.zeros(key_pad.shape, jnp.float32)
    value_acc = jnp.zeros(key_pad.shape, jnp.float32)
    row_ids = jnp.arange(rows_h, dtype=jnp.int32)
    col_ids = jnp.arange(rows_w, dtype=jnp.int32)
    for row_off in range(3):
        for col_off in range(3):
            key_tiles = key_pad[row_off:row_off + rows_h, col_off:col_off + rows_w]
            value_tiles = value_pad[row_off:row_off + rows_h, col_off:col_off + rows_w]
            glob_h = row_ids + row_off - 1
            glob_w = col_ids + col_off - 1
            inside_h = (glob_h >= 0) & (glob_h < rows_h)
            inside_w = (glob_w >= 0) & (glob_w < rows_w)
            valid = (inside_h[:, None] & inside_w[None, :]).astype(jnp.float32)
            scores = jnp.einsum("abqd,abkd->abqk", query_f, key_tiles) * softmax_scale
            probs = jnp.exp(scores - norm_h[..., None]) * valid[:, :, None, None]
            probs_bf = probs.astype(jnp.bfloat16).astype(jnp.float32)
            value_acc = value_acc.at[row_off:row_off + rows_h, col_off:col_off + rows_w].add(
                jnp.einsum("abqk,abqd->abkd", probs_bf, grad_f))
            grad_probs = jnp.einsum("abqd,abkd->abqk", grad_f, value_tiles)
            grad_scores = (probs * (grad_probs - dots_h[..., None]) * softmax_scale).astype(jnp.bfloat16).astype(jnp.float32)
            grad_q = grad_q + jnp.einsum("abqk,abkd->abqd", grad_scores, key_tiles)
            key_acc = key_acc.at[row_off:row_off + rows_h, col_off:col_off + rows_w].add(
                jnp.einsum("abqk,abqd->abkd", grad_scores, query_f))
    return (grad_q.astype(jnp.bfloat16),
            key_acc[1:-1, 1:-1].astype(jnp.bfloat16),
            value_acc[1:-1, 1:-1].astype(jnp.bfloat16))


def reference(query_in, key_in, value_in, out_fwd, grad_out, log_norm):
    rows_h, rows_w, tile_len, chan_all = query_in.shape
    heads_all = chan_all // HD

    def by_head(block):
        return block.reshape(rows_h, rows_w, tile_len, heads_all, HD).transpose(3, 0, 1, 2, 4)

    products = grad_out.astype(jnp.float32) * out_fwd.astype(jnp.float32)
    row_dots = jnp.sum(products.reshape(rows_h, rows_w, tile_len, heads_all, HD), axis=-1)
    results = lax.map(one_head, (by_head(query_in), by_head(key_in), by_head(value_in), by_head(grad_out),
                                 log_norm.transpose(3, 0, 1, 2), row_dots.transpose(3, 0, 1, 2)))

    def back(block):
        return block.transpose(1, 2, 3, 0, 4).reshape(rows_h, rows_w, tile_len, chan_all)

    return (back(results[0]), back(results[1]), back(results[2]))
```

```python
import jax
import jax.numpy as jnp
from jax import lax
from jax.experimental import pallas as pl
from jax.experimental.pallas import tpu as pltpu
from jax.sharding import PartitionSpec as P

HD = 128
MESH = pl.DeviceIdType.MESH
F32 = jnp.float32
BF16 = jnp.bfloat16
NT = (((1,), (1,)), ((), ()))
NN = (((1,), (0,)), ((), ()))


def dot(a, b, dims):
    return lax.dot_general(a, b, dims, preferred_element_type=F32)


def body(
    nh, nw, nd, heads, tok,
    q_hbm, k_hbm, v_hbm, o_hbm, g_hbm, n_hbm,
    res,
    xin, o_in, n_in, qd, kv, pad, st_out, st_in, st,
    k_t, dq_acc, kv_acc, rq_send, rq_recv, rk_send, rk_recv, out_send,
    sem_load, s_in, r_in, s_st, r_st, s_z, r_z, s_x, r_x, s_sz, r_sz,
    s_rq, r_rq, s_rk, r_rk, s_out, r_out,
):
    ih, iw, me = lax.axis_index("ha"), lax.axis_index("wa"), lax.axis_index("hd")
    tile = nd * tok
    scale = HD ** -0.5
    sides_h = (("ha", ih > 0, ih - 1, 0, 2), ("ha", ih < nh - 1, ih + 1, 2, 0))
    sides_w = (("wa", iw > 0, iw - 1, 0, 2), ("wa", iw < nw - 1, iw + 1, 2, 0))

    barrier = pltpu.get_barrier_semaphore()

    def greet(t, c):
        pl.semaphore_signal(barrier, inc=1, device_id={"hd": lax.rem(me + 1 + t, nd)}, device_id_type=MESH)
        return c

    lax.fori_loop(0, nd - 1, greet, 0)
    for axis, exists, other, _, _ in sides_h + sides_w:
        @pl.when(exists)
        def _():
            pl.semaphore_signal(barrier, inc=1, device_id={axis: other}, device_id_type=MESH)

    loads = [
        pltpu.make_async_copy(src, dst, sem_load.at[n])
        for n, (src, dst) in enumerate((
            (q_hbm, xin.at[0]), (g_hbm, xin.at[1]), (k_hbm, xin.at[2]), (v_hbm, xin.at[3]),
            (o_hbm, o_in), (n_hbm, n_in),
        ))
    ]
    for load in loads:
        load.start()

    for _, exists, _, slot, _ in sides_h:
        @pl.when(jnp.logical_not(exists))
        def _():
            qd[slot] = jnp.zeros(qd.shape[1:], BF16)
            st[slot] = jnp.zeros(st.shape[1:], F32)
            rq_recv[slot // 2] = jnp.zeros(rq_recv.shape[1:], BF16)
    for _, exists, _, slot, _ in sides_w:
        @pl.when(jnp.logical_not(exists))
        def _():
            kv[slot] = jnp.zeros(kv.shape[1:], BF16)
            rk_recv[slot // 2] = jnp.zeros(rk_recv.shape[1:], BF16)

    for load in loads[:4]:
        load.wait()
    count = jnp.int32(nd - 1)
    for _, exists, _, _, _ in sides_h + sides_w:
        count = count + exists.astype(jnp.int32)
    pl.semaphore_wait(barrier, count)

    my_rows = pl.ds(pl.multiple_of(me * tok, tok), tok)

    def spread(h, part, dst):
        def lanes(d):
            return pl.ds(pl.multiple_of(d * (heads * HD) + h * HD, HD), HD)

        def one(t, c):
            d = lax.rem(me + 1 + t, nd)
            pltpu.make_async_remote_copy(
                src_ref=xin.at[pl.ds(2 * part, 2), :, lanes(d)],
                dst_ref=dst.at[1, h, :, my_rows, :],
                send_sem=s_in.at[h, part, t], recv_sem=r_in.at[h, part],
                device_id={"hd": d}, device_id_type=MESH,
            ).start()
            return c

        lax.fori_loop(0, nd - 1, one, 0)
        pltpu.make_async_copy(
            xin.at[pl.ds(2 * part, 2), :, lanes(me)], dst.at[1, h, :, my_rows, :], r_in.at[h, part]
        ).start()

    for h in range(heads):
        spread(h, 0, qd)
        spread(h, 1, kv)

    for load in loads[4:]:
        load.wait()
    lane = lax.broadcasted_iota(jnp.int32, (tok, 128), 1)
    table = jnp.zeros((tok, 128), F32)
    norms = n_in[...]
    for g in range(nd * heads):
        d, h = g // heads, g % heads
        cols = slice(g * HD, (g + 1) * HD)
        dots = jnp.sum(xin[1, :, cols].astype(F32) * o_in[:, cols].astype(F32), axis=1, keepdims=True)
        table = jnp.where(lane == 8 * d + h, norms[:, g:g + 1], table)
        table = jnp.where(lane == 8 * d + heads + h, dots, table)
    pad[...] = jnp.zeros(pad.shape, F32)
    pad[pl.ds(pl.multiple_of(lax.rem(me, 4) * tok, tok), tok), :] = table
    st_out[...] = pad[...].T

    def spread_stats(t, c):
        d = lax.rem(me + 1 + t, nd)
        pltpu.make_async_remote_copy(
            src_ref=st_out.at[pl.ds(pl.multiple_of(d * 8, 8), 8), :], dst_ref=st_in.at[me],
            send_sem=s_st.at[t], recv_sem=r_st.at[0], device_id={"hd": d}, device_id_type=MESH,
        ).start()
        return c

    lax.fori_loop(0, nd - 1, spread_stats, 0)
    pltpu.make_async_copy(
        st_out.at[pl.ds(pl.multiple_of(me * 8, 8), 8), :], st_in.at[me], r_st.at[0]
    ).start()

    def halo(buf, h, side, send, recv):
        axis, _, other, slot, there = side
        return pltpu.make_async_remote_copy(
            src_ref=buf.at[1, h], dst_ref=buf.at[there, h],
            send_sem=send.at[h, slot // 2], recv_sem=recv.at[h, there // 2],
            device_id={axis: other}, device_id_type=MESH,
        )

    def halo_stats(side):
        axis, _, other, slot, there = side
        return pltpu.make_async_remote_copy(
            src_ref=st.at[1], dst_ref=st.at[there],
            send_sem=s_sz.at[slot // 2], recv_sem=r_sz.at[there // 2],
            device_id={axis: other}, device_id_type=MESH,
        )

    def when(side, fn):
        @pl.when(side[1])
        def _():
            fn()

    for h in range(heads):
        pltpu.make_async_copy(qd.at[1, h], qd.at[1, h], r_in.at[h, 0]).wait()
        for side in sides_h:
            when(side, lambda: halo(qd, h, side, s_z, r_z).start())
        pltpu.make_async_copy(kv.at[1, h], kv.at[1, h], r_in.at[h, 1]).wait()
        for side in sides_w:
            when(side, lambda: halo(kv, h, side, s_x, r_x).start())
        if h == 0:
            pltpu.make_async_copy(st_in, st_in, r_st.at[0]).wait()
            got = st_in[...]
            st[1] = jnp.concatenate(
                [got[0] + got[1] + got[2] + got[3], got[4] + got[5] + got[6] + got[7]], axis=1
            )
            for side in sides_h:
                when(side, lambda: halo_stats(side).start())

    def arrived(buf, slot, h, sem):
        pltpu.make_async_copy(buf.at[slot, h], buf.at[slot, h], sem.at[h, slot // 2]).wait()

    def back_q(h, side):
        axis, _, other, slot, there = side
        return pltpu.make_async_remote_copy(
            src_ref=rq_send.at[slot // 2, h], dst_ref=rq_recv.at[there // 2, h],
            send_sem=s_rq.at[slot // 2, h], recv_sem=r_rq.at[there // 2, h],
            device_id={axis: other}, device_id_type=MESH,
        )

    def back_kv(h, side):
        axis, _, other, slot, there = side
        return pltpu.make_async_remote_copy(
            src_ref=rk_send.at[slot // 2, h], dst_ref=rk_recv.at[there // 2, h],
            send_sem=s_rk.at[slot // 2, h], recv_sem=r_rk.at[there // 2, h],
            device_id={axis: other}, device_id_type=MESH,
        )

    def out_copy(h, t):
        d = lax.rem(me + 1 + t, nd)
        return pltpu.make_async_remote_copy(
            src_ref=out_send.at[h, :, pl.ds(pl.multiple_of(d * tok, tok), tok), :],
            dst_ref=res.at[:, :, pl.ds(pl.multiple_of(me * (heads * HD) + h * HD, HD), HD)],
            send_sem=s_out.at[h, t], recv_sem=r_out.at[h],
            device_id={"hd": d}, device_id_type=MESH,
        )

    def compute(h):
        for side in sides_w:
            when(side, lambda: arrived(kv, side[3], h, r_x))
        for b in range(3):
            k_t[b] = kv[b, h, 0].T
        for n, a in enumerate((1, 0, 2)):
            if a != 1:
                side = sides_h[a // 2]
                when(side, lambda: arrived(qd, a, h, r_z))

                @pl.when(side[1] & (h == 0))
                def _():
                    pltpu.make_async_copy(st.at[a], st.at[a], r_sz.at[a // 2]).wait()
            q, g = qd[a, h, 0], qd[a, h, 1]
            norm = st[a, pl.ds(h, 1), :]
            dots = st[a, pl.ds(heads + h, 1), :]
            dq = None
            for b in range(3):
                s_t = dot(kv[b, h, 0], q, NT)
                p_t = jnp.exp(s_t * scale - norm)
                dp_t = dot(kv[b, h, 1], g, NT)
                ds_t = (p_t * (dp_t - dots) * scale).astype(BF16)
                dk = dot(ds_t, q, NN)
                dv = dot(p_t.astype(BF16), g, NN)
                term = dot(k_t[b], ds_t, NN)
                dq = term if dq is None else dq + term
                if n == 0:
                    kv_acc[h, b, 0] = dk
                    kv_acc[h, b, 1] = dv
                else:
                    kv_acc[h, b, 0] += dk
                    kv_acc[h, b, 1] += dv
            if a == 1:
                dq_acc[h] = dq
            else:
                rq_send[a // 2, h] = dq.astype(BF16)
                when(sides_h[a // 2], lambda: back_q(h, sides_h[a // 2]).start())
        for side in sides_w:
            slot = side[3]
            rk_send[slot // 2, h] = kv_acc[h, slot].astype(BF16)
            when(side, lambda: back_kv(h, side).start())

    def finish(h):
        for n, side in enumerate(sides_h):
            when(side, lambda: pltpu.make_async_copy(
                rq_recv.at[n, h], rq_recv.at[n, h], r_rq.at[n, h]).wait())
        for n, side in enumerate(sides_w):
            when(side, lambda: pltpu.make_async_copy(
                rk_recv.at[n, h], rk_recv.at[n, h], r_rk.at[n, h]).wait())
        dq = dq_acc[h] + rq_recv[0, h].astype(F32) + rq_recv[1, h].astype(F32)
        out_send[h, 0] = dq.T.astype(BF16)
        for n in range(2):
            out_send[h, 1 + n] = (
                kv_acc[h, 1, n] + rk_recv[0, h, n].astype(F32) + rk_recv[1, h, n].astype(F32)
            ).astype(BF16)

        def one(t, c):
            out_copy(h, t).start()
            return c

        lax.fori_loop(0, nd - 1, one, 0)
        pltpu.make_async_copy(
            out_send.at[h, :, my_rows, :],
            res.at[:, :, pl.ds(pl.multiple_of(me * (heads * HD) + h * HD, HD), HD)],
            r_out.at[h],
        ).start()

    def step(h, c):
        compute(h)

        @pl.when(h > 0)
        def _():
            finish(h - 1)
        return c

    lax.fori_loop(0, heads, step, 0)
    finish(heads - 1)

    def drain(t, c):
        d = lax.rem(me + 1 + t, nd)
        for h in range(heads):
            for part in range(2):
                src = xin.at[pl.ds(2 * part, 2), :, pl.ds(0, HD)]
                pltpu.make_async_copy(src, src, s_in.at[h, part, t]).wait()
            src = out_send.at[h, :, pl.ds(0, tok), :]
            pltpu.make_async_copy(src, src, s_out.at[h, t]).wait()
        src = st_out.at[pl.ds(0, 8), :]
        pltpu.make_async_copy(src, src, s_st.at[t]).wait()
        return c

    lax.fori_loop(0, nd - 1, drain, 0)
    for side in sides_h:
        when(side, lambda: halo_stats(side).wait_send())
    for h in range(heads):
        for side in sides_h:
            when(side, lambda: halo(qd, h, side, s_z, r_z).wait_send())
            when(side, lambda: back_q(h, side).wait_send())
        for side in sides_w:
            when(side, lambda: halo(kv, h, side, s_x, r_x).wait_send())
            when(side, lambda: back_kv(h, side).wait_send())
    for h in range(heads):
        part = res.at[:, :, pl.ds(0, nd * HD)]
        pltpu.make_async_copy(part, part, r_out.at[h]).wait()


def solution(mesh):
    nh, nw, nd = mesh.shape["ha"], mesh.shape["wa"], mesh.shape["hd"]
    spec = P("ha", "wa", "hd", None)

    def per_device(q, k, v, o, g, n):
        tok, chan = q.shape[2], q.shape[3]
        heads = chan // HD // nd
        tile = tok * nd
        lead = q.shape

        def kernel(*refs):
            body(nh, nw, nd, heads, tok, *refs)

        dma = pltpu.SemaphoreType.DMA
        res = pl.pallas_call(
            kernel,
            out_shape=jax.ShapeDtypeStruct((3, tok, chan), BF16),
            in_specs=[pl.BlockSpec(memory_space=pl.ANY)] * 6,
            out_specs=pl.BlockSpec(memory_space=pltpu.VMEM),
            scratch_shapes=[
                pltpu.VMEM((4, tok, chan), BF16),
                pltpu.VMEM((tok, chan), BF16),
                pltpu.VMEM((tok, n.shape[3]), F32),
                pltpu.VMEM((3, heads, 2, tile, HD), BF16),
                pltpu.VMEM((3, heads, 2, tile, HD), BF16),
                pltpu.VMEM((128, 128), F32),
                pltpu.VMEM((128, 128), F32),
                pltpu.VMEM((nd, 8, 128), F32),
                pltpu.VMEM((3, 8, tile), F32),
                pltpu.VMEM((3, HD, tile), BF16),
                pltpu.VMEM((heads, HD, tile), F32),
                pltpu.VMEM((heads, 3, 2, tile, HD), F32),
                pltpu.VMEM((2, heads, HD, tile), BF16),
                pltpu.VMEM((2, heads, HD, tile), BF16),
                pltpu.VMEM((2, heads, 2, tile, HD), BF16),
                pltpu.VMEM((2, heads, 2, tile, HD), BF16),
                pltpu.VMEM((heads, 3, tile, HD), BF16),
                dma((6,)),
                dma((heads, 2, nd - 1)), dma((heads, 2)),
                dma((nd - 1,)), dma((1,)),
                dma((heads, 2)), dma((heads, 2)),
                dma((heads, 2)), dma((heads, 2)),
                dma((2,)), dma((2,)),
                dma((2, heads)), dma((2, heads)),
                dma((2, heads)), dma((2, heads)),
                dma((heads, nd - 1)), dma((heads,)),
            ],
            compiler_params=pltpu.CompilerParams(
                collective_id=0, has_side_effects=True, vmem_limit_bytes=48 * 1024 * 1024
            ),
        )(*(x.reshape(x.shape[2:]) for x in (q, k, v, o, g, n)))
        return tuple(res[i].reshape(lead) for i in range(3))

    return jax.shard_map(
        per_device, mesh=mesh, in_specs=(spec,) * 6, out_specs=(spec,) * 3, check_vma=False
    )
```

```python
import jax
import jax.numpy as jnp
from jax import lax
from jax.experimental import pallas as pl
from jax.experimental.pallas import tpu as pltpu
from jax.sharding import PartitionSpec as P

HD = 128
MESH = pl.DeviceIdType.MESH
F32 = jnp.float32
BF16 = jnp.bfloat16
NT = (((1,), (1,)), ((), ()))
NN = (((1,), (0,)), ((), ()))


def dot(a, b, dims):
    return lax.dot_general(a, b, dims, preferred_element_type=F32)


def body(
    nh, nw, nd, heads, tok,
    q_hbm, k_hbm, v_hbm, o_hbm, g_hbm, n_hbm,
    res,
    xin, o_in, n_in, n_out, qd, kv, pad, st_out, st_in, st,
    k_t, dq_acc, kv_acc, rq_send, rq_recv, rk_send, rk_recv, out_send, relay,
    sem_load, s_in, r_in, s_st, r_st, s_z, r_z, s_x, r_x, s_sz, r_sz,
    s_rq, r_rq, s_rk, r_rk, s_out, r_out, s_relay, r_relay,
):
    ih, iw, me = lax.axis_index("ha"), lax.axis_index("wa"), lax.axis_index("hd")
    tile = nd * tok
    scale = HD ** -0.5
    sides_h = (("ha", ih > 0, ih - 1, 0, 2), ("ha", ih < nh - 1, ih + 1, 2, 0))
    sides_w = (("wa", iw > 0, iw - 1, 0, 2), ("wa", iw < nw - 1, iw + 1, 2, 0))
    mid = nw // 2
    detours = ((mid - 1, 0, mid, 0), (mid, nw - 1, mid - 1, 2))
    at_mid, at_end = (iw == mid - 1) | (iw == mid), (iw == 0) | (iw == nw - 1)

    barrier = pltpu.get_barrier_semaphore()

    def greet(t, c):
        pl.semaphore_signal(barrier, inc=1, device_id={"hd": lax.rem(me + 1 + t, nd)}, device_id_type=MESH)
        return c

    lax.fori_loop(0, nd - 1, greet, 0)
    for axis, exists, other, _, _ in sides_h + sides_w:
        @pl.when(exists)
        def _():
            pl.semaphore_signal(barrier, inc=1, device_id={axis: other}, device_id_type=MESH)
    for there, others in ((at_mid, (0, nw - 1)), (at_end, (mid - 1, mid))):
        @pl.when(there)
        def _():
            for other in others:
                pl.semaphore_signal(barrier, inc=1, device_id={"wa": other}, device_id_type=MESH)

    loads = [
        pltpu.make_async_copy(src, dst, sem_load.at[n])
        for n, (src, dst) in enumerate((
            (q_hbm, xin.at[0]), (g_hbm, xin.at[1]), (k_hbm, xin.at[2]), (v_hbm, xin.at[3]),
            (o_hbm, o_in), (n_hbm, n_in),
        ))
    ]
    for load in loads:
        load.start()

    for _, exists, _, slot, _ in sides_h:
        @pl.when(jnp.logical_not(exists))
        def _():
            qd[slot] = jnp.zeros(qd.shape[1:], BF16)
            st[slot] = jnp.zeros(st.shape[1:], F32)
            rq_recv[slot // 2] = jnp.zeros(rq_recv.shape[1:], BF16)
    for _, exists, _, slot, _ in sides_w:
        @pl.when(jnp.logical_not(exists))
        def _():
            kv[slot] = jnp.zeros(kv.shape[1:], BF16)
            rk_recv[slot // 2] = jnp.zeros(rk_recv.shape[1:], BF16)

    for load in loads[:4]:
        load.wait()
    count = jnp.int32(nd - 1)
    for _, exists, _, _, _ in sides_h + sides_w:
        count = count + exists.astype(jnp.int32)
    count = count + 2 * (at_mid | at_end).astype(jnp.int32)
    pl.semaphore_wait(barrier, count)

    my_rows = pl.ds(pl.multiple_of(me * tok, tok), tok)

    def spread(h, part, dst):
        def lanes(d):
            return pl.ds(pl.multiple_of(d * (heads * HD) + h * HD, HD), HD)

        def one(t, c):
            d = lax.rem(me + 1 + t, nd)
            pltpu.make_async_remote_copy(
                src_ref=xin.at[pl.ds(2 * part, 2), :, lanes(d)],
                dst_ref=dst.at[1, h, :, my_rows, :],
                send_sem=s_in.at[h, part, t], recv_sem=r_in.at[h, part],
                device_id={"hd": d}, device_id_type=MESH,
            ).start()
            return c

        lax.fori_loop(0, nd - 1, one, 0)
        pltpu.make_async_copy(
            xin.at[pl.ds(2 * part, 2), :, lanes(me)], dst.at[1, h, :, my_rows, :], r_in.at[h, part]
        ).start()

    for h in range(heads):
        spread(h, 0, qd)
        spread(h, 1, kv)

    for load in loads[4:]:
        load.wait()
    lane = lax.broadcasted_iota(jnp.int32, (tok, 128), 1)
    table = jnp.zeros((tok, 128), F32)
    n_out[...] = jnp.zeros(n_out.shape, F32)
    for g in range(nd * heads):
        d, h = g // heads, g % heads
        cols = slice(g * HD, (g + 1) * HD)
        dots = jnp.sum(xin[1, :, cols].astype(F32) * o_in[:, cols].astype(F32), axis=1, keepdims=True)
        n_out[8 * d + h:8 * d + h + 1, :tok] = n_in[g:g + 1, :]
        table = jnp.where(lane == 8 * d + heads + h, dots, table)
    pad[...] = jnp.zeros(pad.shape, F32)
    pad[pl.ds(pl.multiple_of(lax.rem(me, 4) * tok, tok), tok), :] = table
    st_out[...] = pad[...].T[:64] + pltpu.roll(n_out[...], lax.rem(me, 4) * tok, 1)

    def spread_stats(t, c):
        d = lax.rem(me + 1 + t, nd)
        pltpu.make_async_remote_copy(
            src_ref=st_out.at[pl.ds(pl.multiple_of(d * 8, 8), 8), :], dst_ref=st_in.at[me],
            send_sem=s_st.at[t], recv_sem=r_st.at[0], device_id={"hd": d}, device_id_type=MESH,
        ).start()
        return c

    lax.fori_loop(0, nd - 1, spread_stats, 0)
    pltpu.make_async_copy(
        st_out.at[pl.ds(pl.multiple_of(me * 8, 8), 8), :], st_in.at[me], r_st.at[0]
    ).start()

    def halo(buf, h, side, send, recv):
        axis, _, other, slot, there = side
        return pltpu.make_async_remote_copy(
            src_ref=buf.at[1, h], dst_ref=buf.at[there, h],
            send_sem=send.at[h, slot // 2], recv_sem=recv.at[h, there // 2],
            device_id={axis: other}, device_id_type=MESH,
        )

    def seam(side):
        return at_mid & (side[2] == (2 * mid - 1) - iw)

    def leg(src, dst, send, recv, to):
        return pltpu.make_async_remote_copy(
            src_ref=src, dst_ref=dst, send_sem=send, recv_sem=recv,
            device_id={"wa": to}, device_id_type=MESH,
        )

    def send_kv(h, side, src, dst, send, recv, trip):
        @pl.when(side[1] & jnp.logical_not(seam(side)))
        def _():
            leg(src, dst, send, recv, side[2]).start()

        @pl.when(side[1] & seam(side))
        def _():
            leg(src.at[0], dst.at[0], send, recv, side[2]).start()
            leg(src.at[1], relay.at[trip, h], send, r_relay.at[trip, h], detour_of(side)).start()

    def detour_of(side):
        return jnp.where(iw == mid - 1, detours[0][1], detours[1][1])

    def pass_on(h, buf_of, sem_of, trip):
        for _, via, target, there in detours:
            @pl.when(iw == via)
            def _():
                pltpu.make_async_copy(relay.at[trip, h], relay.at[trip, h], r_relay.at[trip, h]).wait()
                leg(relay.at[trip, h], buf_of(there).at[1], s_relay.at[trip, h], sem_of(there), target).start()

    def pass_kv(h):
        pass_on(h, lambda there: kv.at[there, h], lambda there: r_x.at[h, there // 2], 0)

    def pass_back(h):
        pass_on(h, lambda there: rk_recv.at[there // 2, h], lambda there: r_rk.at[there // 2, h], 1)

    def halo_stats(side):
        axis, _, other, slot, there = side
        return pltpu.make_async_remote_copy(
            src_ref=st.at[1], dst_ref=st.at[there],
            send_sem=s_sz.at[slot // 2], recv_sem=r_sz.at[there // 2],
            device_id={axis: other}, device_id_type=MESH,
        )

    def when(side, fn):
        @pl.when(side[1])
        def _():
            fn()

    for h in range(heads):
        pltpu.make_async_copy(qd.at[1, h], qd.at[1, h], r_in.at[h, 0]).wait()
        for side in sides_h:
            when(side, lambda: halo(qd, h, side, s_z, r_z).start())
        pltpu.make_async_copy(kv.at[1, h], kv.at[1, h], r_in.at[h, 1]).wait()
        for side in sides_w:
            send_kv(h, side, kv.at[1, h], kv.at[side[4], h], s_x.at[h, side[3] // 2], r_x.at[h, side[4] // 2], 0)
        if h > 0:
            pass_kv(h - 1)
        if h == 0:
            pltpu.make_async_copy(st_in, st_in, r_st.at[0]).wait()
            got = st_in[...]
            st[1] = jnp.concatenate(
                [got[0] + got[1] + got[2] + got[3], got[4] + got[5] + got[6] + got[7]], axis=1
            )
            for side in sides_h:
                when(side, lambda: halo_stats(side).start())

    pass_kv(heads - 1)

    def arrived(buf, slot, h, sem):
        pltpu.make_async_copy(buf.at[slot, h], buf.at[slot, h], sem.at[h, slot // 2]).wait()

    def back_q(h, side):
        axis, _, other, slot, there = side
        return pltpu.make_async_remote_copy(
            src_ref=rq_send.at[slot // 2, h], dst_ref=rq_recv.at[there // 2, h],
            send_sem=s_rq.at[slot // 2, h], recv_sem=r_rq.at[there // 2, h],
            device_id={axis: other}, device_id_type=MESH,
        )

    def back_kv(h, side):
        axis, _, other, slot, there = side
        return pltpu.make_async_remote_copy(
            src_ref=rk_send.at[slot // 2, h], dst_ref=rk_recv.at[there // 2, h],
            send_sem=s_rk.at[slot // 2, h], recv_sem=r_rk.at[there // 2, h],
            device_id={axis: other}, device_id_type=MESH,
        )

    def out_copy(h, t):
        d = lax.rem(me + 1 + t, nd)
        return pltpu.make_async_remote_copy(
            src_ref=out_send.at[h, :, pl.ds(pl.multiple_of(d * tok, tok), tok), :],
            dst_ref=res.at[:, :, pl.ds(pl.multiple_of(me * (heads * HD) + h * HD, HD), HD)],
            send_sem=s_out.at[h, t], recv_sem=r_out.at[h],
            device_id={"hd": d}, device_id_type=MESH,
        )

    def compute(h):
        for side in sides_w:
            when(side, lambda: arrived(kv, side[3], h, r_x))
        for b in range(3):
            k_t[b] = kv[b, h, 0].T
        for n, a in enumerate((1, 0, 2)):
            if a != 1:
                side = sides_h[a // 2]
                when(side, lambda: arrived(qd, a, h, r_z))

                @pl.when(side[1] & (h == 0))
                def _():
                    pltpu.make_async_copy(st.at[a], st.at[a], r_sz.at[a // 2]).wait()
            q, g = qd[a, h, 0], qd[a, h, 1]
            norm = st[a, pl.ds(h, 1), :]
            dots = st[a, pl.ds(heads + h, 1), :]
            dq = None
            for b in range(3):
                s_t = dot(kv[b, h, 0], q, NT)
                p_t = jnp.exp(s_t * scale - norm)
                dp_t = dot(kv[b, h, 1], g, NT)
                ds_t = (p_t * (dp_t - dots) * scale).astype(BF16)
                dk = dot(ds_t, q, NN)
                dv = dot(p_t.astype(BF16), g, NN)
                term = dot(k_t[b], ds_t, NN)
                dq = term if dq is None else dq + term
                if n == 0:
                    kv_acc[h, b, 0] = dk
                    kv_acc[h, b, 1] = dv
                else:
                    kv_acc[h, b, 0] += dk
                    kv_acc[h, b, 1] += dv
            if a == 1:
                dq_acc[h] = dq
            else:
                rq_send[a // 2, h] = dq.astype(BF16)
                when(sides_h[a // 2], lambda: back_q(h, sides_h[a // 2]).start())
        for side in sides_w:
            slot = side[3]
            rk_send[slot // 2, h] = kv_acc[h, slot].astype(BF16)
            send_kv(
                h, side, rk_send.at[slot // 2, h], rk_recv.at[side[4] // 2, h],
                s_rk.at[slot // 2, h], r_rk.at[side[4] // 2, h], 1,
            )

    def finish(h):
        for n, side in enumerate(sides_h):
            when(side, lambda: pltpu.make_async_copy(
                rq_recv.at[n, h], rq_recv.at[n, h], r_rq.at[n, h]).wait())
        for n, side in enumerate(sides_w):
            when(side, lambda: pltpu.make_async_copy(
                rk_recv.at[n, h], rk_recv.at[n, h], r_rk.at[n, h]).wait())
        dq = dq_acc[h] + rq_recv[0, h].astype(F32) + rq_recv[1, h].astype(F32)
        out_send[h, 0] = dq.T.astype(BF16)
        for n in range(2):
            out_send[h, 1 + n] = (
                kv_acc[h, 1, n] + rk_recv[0, h, n].astype(F32) + rk_recv[1, h, n].astype(F32)
            ).astype(BF16)

        def one(t, c):
            out_copy(h, t).start()
            return c

        lax.fori_loop(0, nd - 1, one, 0)
        pltpu.make_async_copy(
            out_send.at[h, :, my_rows, :],
            res.at[:, :, pl.ds(pl.multiple_of(me * (heads * HD) + h * HD, HD), HD)],
            r_out.at[h],
        ).start()

    def step(h, c):
        compute(h)

        @pl.when(h > 0)
        def _():
            pass_back(h - 1)
        return c

    lax.fori_loop(0, heads, step, 0)
    pass_back(heads - 1)

    def close(h, c):
        finish(h)
        return c

    lax.fori_loop(0, heads, close, 0)

    def drain(t, c):
        d = lax.rem(me + 1 + t, nd)
        for h in range(heads):
            for part in range(2):
                src = xin.at[pl.ds(2 * part, 2), :, pl.ds(0, HD)]
                pltpu.make_async_copy(src, src, s_in.at[h, part, t]).wait()
            src = out_send.at[h, :, pl.ds(0, tok), :]
            pltpu.make_async_copy(src, src, s_out.at[h, t]).wait()
        src = st_out.at[pl.ds(0, 8), :]
        pltpu.make_async_copy(src, src, s_st.at[t]).wait()
        return c

    lax.fori_loop(0, nd - 1, drain, 0)
    for side in sides_h:
        when(side, lambda: halo_stats(side).wait_send())
    for h in range(heads):
        for side in sides_h:
            when(side, lambda: halo(qd, h, side, s_z, r_z).wait_send())
            when(side, lambda: back_q(h, side).wait_send())
        for side in sides_w:
            when(side, lambda: halo(kv, h, side, s_x, r_x).wait_send())
            when(side, lambda: back_kv(h, side).wait_send())

        @pl.when(at_end)
        def _():
            for trip in range(2):
                pltpu.make_async_copy(relay.at[trip, h], relay.at[trip, h], s_relay.at[trip, h]).wait()
    for h in range(heads):
        part = res.at[:, :, pl.ds(0, nd * HD)]
        pltpu.make_async_copy(part, part, r_out.at[h]).wait()


def solution(mesh):
    nh, nw, nd = mesh.shape["ha"], mesh.shape["wa"], mesh.shape["hd"]
    spec = P("ha", "wa", "hd", None)

    def per_device(q, k, v, o, g, n):
        tok, chan = q.shape[2], q.shape[3]
        heads = chan // HD // nd
        tile = tok * nd
        lead = q.shape

        def kernel(*refs):
            body(nh, nw, nd, heads, tok, *refs)

        dma = pltpu.SemaphoreType.DMA
        res = pl.pallas_call(
            kernel,
            out_shape=jax.ShapeDtypeStruct((3, tok, chan), BF16),
            in_specs=[pl.BlockSpec(memory_space=pltpu.HBM)] * 6,
            out_specs=pl.BlockSpec(memory_space=pltpu.HBM),
            scratch_shapes=[
                pltpu.VMEM((4, tok, chan), BF16),
                pltpu.VMEM((tok, chan), BF16),
                pltpu.VMEM((n.shape[3], tok), F32),
                pltpu.VMEM((64, 128), F32),
                pltpu.VMEM((3, heads, 2, tile, HD), BF16),
                pltpu.VMEM((3, heads, 2, tile, HD), BF16),
                pltpu.VMEM((128, 128), F32),
                pltpu.VMEM((64, 128), F32),
                pltpu.VMEM((nd, 8, 128), F32),
                pltpu.VMEM((3, 8, tile), F32),
                pltpu.VMEM((3, HD, tile), BF16),
                pltpu.VMEM((heads, HD, tile), F32),
                pltpu.VMEM((heads, 3, 2, tile, HD), F32),
                pltpu.VMEM((2, heads, HD, tile), BF16),
                pltpu.VMEM((2, heads, HD, tile), BF16),
                pltpu.VMEM((2, heads, 2, tile, HD), BF16),
                pltpu.VMEM((2, heads, 2, tile, HD), BF16),
                pltpu.VMEM((heads, 3, tile, HD), BF16),
                pltpu.VMEM((2, heads, tile, HD), BF16),
                dma((6,)),
                dma((heads, 2, nd - 1)), dma((heads, 2)),
                dma((nd - 1,)), dma((1,)),
                dma((heads, 2)), dma((heads, 2)),
                dma((heads, 2)), dma((heads, 2)),
                dma((2,)), dma((2,)),
                dma((2, heads)), dma((2, heads)),
                dma((2, heads)), dma((2, heads)),
                dma((heads, nd - 1)), dma((heads,)),
                dma((2, heads)), dma((2, heads)),
            ],
            compiler_params=pltpu.CompilerParams(
                collective_id=0, has_side_effects=True, vmem_limit_bytes=60 * 1024 * 1024
            ),
        )(*(x.reshape(x.shape[2:]) for x in (q, k, v, o, g)), n.reshape(n.shape[2:]).T)
        return tuple(res[i].reshape(lead) for i in range(3))

    return jax.shard_map(
        per_device, mesh=mesh, in_specs=(spec,) * 6, out_specs=(spec,) * 3, check_vma=False
    )
```

```python
import jax
import jax.numpy as jnp
from jax import lax
from jax.experimental import pallas as pl
from jax.experimental.pallas import tpu as pltpu
from jax.sharding import PartitionSpec as P

HD = 128
FAR = ((1, 1, 1), (1, 1, 1))
MESH = pl.DeviceIdType.MESH
F32 = jnp.float32
BF16 = jnp.bfloat16
NT = (((1,), (1,)), ((), ()))
NN = (((1,), (0,)), ((), ()))


def dot(a, b, dims):
    return lax.dot_general(a, b, dims, preferred_element_type=F32)


def body(
    nh, nw, nd, heads, tok,
    q_hbm, k_hbm, v_hbm, o_hbm, g_hbm, n_hbm,
    res,
    xin, o_in, n_in, n_out, qd, kv, pad, st_out, st_in, st,
    k_t, dq_acc, kv_acc, rq_send, rq_recv, rk_send, rk_recv, out_send, relay, raw,
    sem_load, s_in, r_in, s_st, r_st, s_z, r_z, s_x, r_x, s_sz, r_sz,
    s_rq, r_rq, s_rk, r_rk, s_out, r_out, s_relay, r_relay, s_raw, r_raw, s_spread,
):
    ih, iw, me = lax.axis_index("ha"), lax.axis_index("wa"), lax.axis_index("hd")
    tile = nd * tok
    scale = HD ** -0.5
    sides_h = (("ha", ih > 0, ih - 1, 0, 2), ("ha", ih < nh - 1, ih + 1, 2, 0))
    sides_w = (("wa", iw > 0, iw - 1, 0, 2), ("wa", iw < nw - 1, iw + 1, 2, 0))
    mid = nw // 2
    detours = ((mid - 1, 0, mid, 0), (mid, nw - 1, mid - 1, 2))
    at_mid, at_end = (iw == mid - 1) | (iw == mid), (iw == 0) | (iw == nw - 1)

    barrier = pltpu.get_barrier_semaphore()

    def greet(t, c):
        pl.semaphore_signal(barrier, inc=1, device_id={"hd": lax.rem(me + 1 + t, nd)}, device_id_type=MESH)
        return c

    lax.fori_loop(0, nd - 1, greet, 0)
    for axis, exists, other, _, _ in sides_h + sides_w:
        @pl.when(exists)
        def _():
            pl.semaphore_signal(barrier, inc=1, device_id={axis: other}, device_id_type=MESH)
    for there, others in ((at_mid, (0, nw - 1)), (at_end, (mid - 1, mid))):
        @pl.when(there)
        def _():
            for other in others:
                pl.semaphore_signal(barrier, inc=1, device_id={"wa": other}, device_id_type=MESH)

    loads = [
        pltpu.make_async_copy(src, dst, sem_load.at[n])
        for n, (src, dst) in enumerate((
            (q_hbm, xin.at[0]), (g_hbm, xin.at[1]), (k_hbm, xin.at[2]), (v_hbm, xin.at[3]),
            (o_hbm, o_in), (n_hbm, n_in),
        ))
    ]
    for load in loads:
        load.start()

    for _, exists, _, slot, _ in sides_h:
        @pl.when(jnp.logical_not(exists))
        def _():
            qd[slot] = jnp.zeros(qd.shape[1:], BF16)
            st[slot] = jnp.zeros(st.shape[1:], F32)
            rq_recv[slot // 2] = jnp.zeros(rq_recv.shape[1:], BF16)
    for _, exists, _, slot, _ in sides_w:
        @pl.when(jnp.logical_not(exists))
        def _():
            kv[slot] = jnp.zeros(kv.shape[1:], BF16)
            rk_recv[slot // 2] = jnp.zeros(rk_recv.shape[1:], BF16)

    for load in loads[:4]:
        load.wait()
    count = jnp.int32(nd - 1)
    for _, exists, _, _, _ in sides_h + sides_w:
        count = count + exists.astype(jnp.int32)
    count = count + 2 * (at_mid | at_end).astype(jnp.int32)
    pl.semaphore_wait(barrier, count)

    def when(side, fn):
        @pl.when(side[1])
        def _():
            fn()

    my_rows = pl.ds(pl.multiple_of(me * tok, tok), tok)

    def spread(h, part, dst):
        def lanes(d):
            return pl.ds(pl.multiple_of((h * nd + d) * HD, HD), HD)

        def one(t, c):
            d = lax.rem(me + 1 + t, nd)
            pltpu.make_async_remote_copy(
                src_ref=xin.at[pl.ds(2 * part, 2), :, lanes(d)],
                dst_ref=dst.at[1, h, :, my_rows, :],
                send_sem=s_in.at[h, part, t], recv_sem=r_in.at[h, part],
                device_id={"hd": d}, device_id_type=MESH,
            ).start()
            return c

        lax.fori_loop(0, nd - 1, one, 0)
        pltpu.make_async_copy(
            xin.at[pl.ds(2 * part, 2), :, lanes(me)], dst.at[1, h, :, my_rows, :], r_in.at[h, part]
        ).start()

    def raw_halo(side):
        axis, _, other, slot, there = side
        return pltpu.make_async_remote_copy(
            src_ref=xin.at[pl.ds(0, 2), :, pl.ds(0, nd * HD)], dst_ref=raw.at[there // 2],
            send_sem=s_raw.at[slot // 2], recv_sem=r_raw.at[there // 2],
            device_id={axis: other}, device_id_type=MESH,
        )

    for side in sides_h:
        when(side, lambda: raw_halo(side).start())
    spread(1, 0, qd)
    spread(0, 1, kv)
    spread(0, 0, qd)

    for load in loads[4:]:
        load.wait()
    lane = lax.broadcasted_iota(jnp.int32, (tok, 128), 1)
    table = jnp.zeros((tok, 128), F32)
    n_out[...] = jnp.zeros(n_out.shape, F32)
    for g in range(nd * heads):
        h, d = g // nd, g % nd
        cols = slice(g * HD, (g + 1) * HD)
        dots = jnp.sum(xin[1, :, cols].astype(F32) * o_in[:, cols].astype(F32), axis=1, keepdims=True)
        n_out[8 * d + h:8 * d + h + 1, :tok] = n_in[g:g + 1, :]
        table = jnp.where(lane == 8 * d + heads + h, dots, table)
    pad[...] = jnp.zeros(pad.shape, F32)
    pad[pl.ds(pl.multiple_of(lax.rem(me, 4) * tok, tok), tok), :] = table
    st_out[...] = pad[...].T[:64] + pltpu.roll(n_out[...], lax.rem(me, 4) * tok, 1)

    def spread_stats(t, c):
        d = lax.rem(me + 1 + t, nd)
        pltpu.make_async_remote_copy(
            src_ref=st_out.at[pl.ds(pl.multiple_of(d * 8, 8), 8), :], dst_ref=st_in.at[me],
            send_sem=s_st.at[t], recv_sem=r_st.at[0], device_id={"hd": d}, device_id_type=MESH,
        ).start()
        return c

    lax.fori_loop(0, nd - 1, spread_stats, 0)
    pltpu.make_async_copy(
        st_out.at[pl.ds(pl.multiple_of(me * 8, 8), 8), :], st_in.at[me], r_st.at[0]
    ).start()

    def halo(buf, h, side, send, recv):
        axis, _, other, slot, there = side
        return pltpu.make_async_remote_copy(
            src_ref=buf.at[1, h], dst_ref=buf.at[there, h],
            send_sem=send.at[h, slot // 2], recv_sem=recv.at[h, there // 2],
            device_id={axis: other}, device_id_type=MESH,
        )

    def seam(side):
        return at_mid & (side[2] == (2 * mid - 1) - iw)

    def leg(src, dst, send, recv, to):
        return pltpu.make_async_remote_copy(
            src_ref=src, dst_ref=dst, send_sem=send, recv_sem=recv,
            device_id={"wa": to}, device_id_type=MESH,
        )

    def send_kv(h, side, src, dst, send, recv, trip):
        @pl.when(side[1] & jnp.logical_not(seam(side)))
        def _():
            leg(src, dst, send, recv, side[2]).start()

        @pl.when(side[1] & seam(side))
        def _():
            for n in range(heads):
                @pl.when(h == n)
                def _():
                    near, far = shares(n, trip)
                    if near is not None:
                        leg(src.at[near], dst.at[near], send, recv, side[2]).start()
                    if far is not None:
                        leg(
                            src.at[far], relay.at[trip, n].at[far], send, r_relay.at[trip, n], detour_of(side)
                        ).start()

    def shares(h, trip):
        far = FAR[trip][h]
        return (pl.ds(0, 2 - far) if far < 2 else None), (pl.ds(2 - far, far) if far else None)

    def detour_of(side):
        return jnp.where(iw == mid - 1, detours[0][1], detours[1][1])

    def pass_on(h, buf_of, sem_of, trip):
        far = shares(h, trip)[1]
        if far is None:
            return
        held = relay.at[trip, h].at[far]
        for _, via, target, there in detours:
            @pl.when(iw == via)
            def _():
                pltpu.make_async_copy(held, held, r_relay.at[trip, h]).wait()
                leg(held, buf_of(there).at[far], s_relay.at[trip, h], sem_of(there), target).start()

    def pass_kv(h):
        pass_on(h, lambda there: kv.at[there, h], lambda there: r_x.at[h, there // 2], 0)

    def pass_back(h):
        pass_on(h, lambda there: rk_recv.at[there // 2, h], lambda there: r_rk.at[there // 2, h], 1)

    def halo_stats(side):
        axis, _, other, slot, there = side
        return pltpu.make_async_remote_copy(
            src_ref=st.at[1], dst_ref=st.at[there],
            send_sem=s_sz.at[slot // 2], recv_sem=r_sz.at[there // 2],
            device_id={axis: other}, device_id_type=MESH,
        )

    def spread_raw(side):
        n = side[3] // 2
        pltpu.make_async_copy(raw.at[n], raw.at[n], r_raw.at[n]).wait()

        def one(t, c):
            d = lax.rem(me + 1 + t, nd)
            pltpu.make_async_remote_copy(
                src_ref=raw.at[n, :, :, pl.ds(pl.multiple_of(d * HD, HD), HD)],
                dst_ref=qd.at[side[3], 0, :, my_rows, :],
                send_sem=s_spread.at[n, t], recv_sem=r_z.at[0, n],
                device_id={"hd": d}, device_id_type=MESH,
            ).start()
            return c

        lax.fori_loop(0, nd - 1, one, 0)
        pltpu.make_async_copy(
            raw.at[n, :, :, pl.ds(pl.multiple_of(me * HD, HD), HD)],
            qd.at[side[3], 0, :, my_rows, :], r_z.at[0, n],
        ).start()

    def own(buf, h, part):
        pltpu.make_async_copy(buf.at[1, h], buf.at[1, h], r_in.at[h, part]).wait()

    def send_rows(h):
        own(qd, h, 0)
        for side in sides_h:
            when(side, lambda: halo(qd, h, side, s_z, r_z).start())

    def send_columns(h):
        own(kv, h, 1)
        for side in sides_w:
            send_kv(h, side, kv.at[1, h], kv.at[side[4], h], s_x.at[h, side[3] // 2], r_x.at[h, side[4] // 2], 0)

    send_rows(1)
    for h in range(2, heads):
        spread(h, 0, qd)
    for h in range(1, heads):
        spread(h, 1, kv)
    send_columns(0)
    pltpu.make_async_copy(st_in, st_in, r_st.at[0]).wait()
    got = st_in[...]
    st[1] = jnp.concatenate(
        [got[0] + got[1] + got[2] + got[3], got[4] + got[5] + got[6] + got[7]], axis=1
    )
    for side in sides_h:
        when(side, lambda: halo_stats(side).start())
    for h in range(2, heads):
        send_rows(h)
    for h in range(1, heads):
        send_columns(h)
        if h == 1:
            for side in sides_h:
                when(side, lambda: spread_raw(side))
            own(qd, 0, 0)
        pass_kv(h - 1)
    pass_kv(heads - 1)

    def arrived(buf, slot, h, sem):
        pltpu.make_async_copy(buf.at[slot, h], buf.at[slot, h], sem.at[h, slot // 2]).wait()

    def back_q(h, side):
        axis, _, other, slot, there = side
        return pltpu.make_async_remote_copy(
            src_ref=rq_send.at[slot // 2, h], dst_ref=rq_recv.at[there // 2, h],
            send_sem=s_rq.at[slot // 2, h], recv_sem=r_rq.at[there // 2, h],
            device_id={axis: other}, device_id_type=MESH,
        )

    def back_kv(h, side):
        axis, _, other, slot, there = side
        return pltpu.make_async_remote_copy(
            src_ref=rk_send.at[slot // 2, h], dst_ref=rk_recv.at[there // 2, h],
            send_sem=s_rk.at[slot // 2, h], recv_sem=r_rk.at[there // 2, h],
            device_id={axis: other}, device_id_type=MESH,
        )

    def out_copy(h, t):
        d = lax.rem(me + 1 + t, nd)
        return pltpu.make_async_remote_copy(
            src_ref=out_send.at[h, :, pl.ds(pl.multiple_of(d * tok, tok), tok), :],
            dst_ref=res.at[:, :, pl.ds(pl.multiple_of((h * nd + me) * HD, HD), HD)],
            send_sem=s_out.at[h, t], recv_sem=r_out.at[h],
            device_id={"hd": d}, device_id_type=MESH,
        )

    def compute(h):
        for side in sides_w:
            when(side, lambda: arrived(kv, side[3], h, r_x))
        for b in range(3):
            k_t[b] = kv[b, h, 0].T
        for n, a in enumerate((1, 0, 2)):
            if a != 1:
                side = sides_h[a // 2]
                when(side, lambda: arrived(qd, a, h, r_z))

                @pl.when(side[1] & (h == 0))
                def _():
                    pltpu.make_async_copy(st.at[a], st.at[a], r_sz.at[a // 2]).wait()
            q, g = qd[a, h, 0], qd[a, h, 1]
            norm = st[a, pl.ds(h, 1), :]
            dots = st[a, pl.ds(heads + h, 1), :]
            dq = None
            for b in range(3):
                s_t = dot(kv[b, h, 0], q, NT)
                p_t = jnp.exp(s_t * scale - norm)
                dp_t = dot(kv[b, h, 1], g, NT)
                ds_t = (p_t * (dp_t - dots) * scale).astype(BF16)
                dk = dot(ds_t, q, NN)
                dv = dot(p_t.astype(BF16), g, NN)
                term = dot(k_t[b], ds_t, NN)
                dq = term if dq is None else dq + term
                if n == 0:
                    kv_acc[h, b, 0] = dk
                    kv_acc[h, b, 1] = dv
                else:
                    kv_acc[h, b, 0] += dk
                    kv_acc[h, b, 1] += dv
            if a == 1:
                dq_acc[h] = dq
            else:
                rq_send[a // 2, h] = dq.astype(BF16)
                when(sides_h[a // 2], lambda: back_q(h, sides_h[a // 2]).start())
        for side in sides_w:
            slot = side[3]
            rk_send[slot // 2, h] = kv_acc[h, slot].astype(BF16)
            send_kv(
                h, side, rk_send.at[slot // 2, h], rk_recv.at[side[4] // 2, h],
                s_rk.at[slot // 2, h], r_rk.at[side[4] // 2, h], 1,
            )

    def finish(h):
        for n, side in enumerate(sides_h):
            when(side, lambda: pltpu.make_async_copy(
                rq_recv.at[n, h], rq_recv.at[n, h], r_rq.at[n, h]).wait())
        for n, side in enumerate(sides_w):
            when(side, lambda: pltpu.make_async_copy(
                rk_recv.at[n, h], rk_recv.at[n, h], r_rk.at[n, h]).wait())
        dq = dq_acc[h] + rq_recv[0, h].astype(F32) + rq_recv[1, h].astype(F32)
        out_send[h, 0] = dq.T.astype(BF16)
        for n in range(2):
            out_send[h, 1 + n] = (
                kv_acc[h, 1, n] + rk_recv[0, h, n].astype(F32) + rk_recv[1, h, n].astype(F32)
            ).astype(BF16)

        def one(t, c):
            out_copy(h, t).start()
            return c

        lax.fori_loop(0, nd - 1, one, 0)
        pltpu.make_async_copy(
            out_send.at[h, :, my_rows, :],
            res.at[:, :, pl.ds(pl.multiple_of((h * nd + me) * HD, HD), HD)],
            r_out.at[h],
        ).start()

    def step(h, c):
        compute(h)

        for n in range(1, heads):
            @pl.when(h == n)
            def _():
                pass_back(n - 1)
        return c

    lax.fori_loop(0, heads, step, 0)
    pass_back(heads - 1)

    def close(h, c):
        finish(h)
        return c

    lax.fori_loop(0, heads, close, 0)

    def drain(t, c):
        d = lax.rem(me + 1 + t, nd)
        for h in range(heads):
            for part in range(2):
                src = xin.at[pl.ds(2 * part, 2), :, pl.ds(0, HD)]
                pltpu.make_async_copy(src, src, s_in.at[h, part, t]).wait()
            src = out_send.at[h, :, pl.ds(0, tok), :]
            pltpu.make_async_copy(src, src, s_out.at[h, t]).wait()
        src = st_out.at[pl.ds(0, 8), :]
        pltpu.make_async_copy(src, src, s_st.at[t]).wait()
        return c

    lax.fori_loop(0, nd - 1, drain, 0)
    def drain_raw(side):
        def one(t, c):
            src = raw.at[side[3] // 2, :, :, pl.ds(0, HD)]
            pltpu.make_async_copy(src, src, s_spread.at[side[3] // 2, t]).wait()
            return c

        raw_halo(side).wait_send()
        lax.fori_loop(0, nd - 1, one, 0)

    for side in sides_h:
        when(side, lambda: halo_stats(side).wait_send())
        when(side, lambda: drain_raw(side))
    for h in range(heads):
        for side in sides_h:
            if h > 0:
                when(side, lambda: halo(qd, h, side, s_z, r_z).wait_send())
            when(side, lambda: back_q(h, side).wait_send())
        for side in sides_w:
            when(side, lambda: halo(kv, h, side, s_x, r_x).wait_send())
            when(side, lambda: back_kv(h, side).wait_send())

        @pl.when(at_end)
        def _():
            for trip in range(2):
                far = shares(h, trip)[1]
                if far is not None:
                    held = relay.at[trip, h].at[far]
                    pltpu.make_async_copy(held, held, s_relay.at[trip, h]).wait()
    for h in range(heads):
        part = res.at[:, :, pl.ds(0, nd * HD)]
        pltpu.make_async_copy(part, part, r_out.at[h]).wait()


def solution(mesh):
    nh, nw, nd = mesh.shape["ha"], mesh.shape["wa"], mesh.shape["hd"]
    spec = P("ha", "wa", "hd", None)

    def per_device(q, k, v, o, g, n):
        tok, chan = q.shape[2], q.shape[3]
        heads = chan // HD // nd
        tile = tok * nd
        lead = q.shape

        def kernel(*refs):
            body(nh, nw, nd, heads, tok, *refs)

        dma = pltpu.SemaphoreType.DMA
        res = pl.pallas_call(
            kernel,
            out_shape=jax.ShapeDtypeStruct((3, tok, chan), BF16),
            in_specs=[pl.BlockSpec(memory_space=pltpu.HBM)] * 6,
            out_specs=pl.BlockSpec(memory_space=pltpu.HBM),
            scratch_shapes=[
                pltpu.VMEM((4, tok, chan), BF16),
                pltpu.VMEM((tok, chan), BF16),
                pltpu.VMEM((n.shape[3], tok), F32),
                pltpu.VMEM((64, 128), F32),
                pltpu.VMEM((3, heads, 2, tile, HD), BF16),
                pltpu.VMEM((3, heads, 2, tile, HD), BF16),
                pltpu.VMEM((128, 128), F32),
                pltpu.VMEM((64, 128), F32),
                pltpu.VMEM((nd, 8, 128), F32),
                pltpu.VMEM((3, 8, tile), F32),
                pltpu.VMEM((3, HD, tile), BF16),
                pltpu.VMEM((heads, HD, tile), F32),
                pltpu.VMEM((heads, 3, 2, tile, HD), F32),
                pltpu.VMEM((2, heads, HD, tile), BF16),
                pltpu.VMEM((2, heads, HD, tile), BF16),
                pltpu.VMEM((2, heads, 2, tile, HD), BF16),
                pltpu.VMEM((2, heads, 2, tile, HD), BF16),
                pltpu.VMEM((heads, 3, tile, HD), BF16),
                pltpu.VMEM((2, heads, 2, tile, HD), BF16),
                pltpu.VMEM((2, 2, tok, nd * HD), BF16),
                dma((6,)),
                dma((heads, 2, nd - 1)), dma((heads, 2)),
                dma((nd - 1,)), dma((1,)),
                dma((heads, 2)), dma((heads, 2)),
                dma((heads, 2)), dma((heads, 2)),
                dma((2,)), dma((2,)),
                dma((2, heads)), dma((2, heads)),
                dma((2, heads)), dma((2, heads)),
                dma((heads, nd - 1)), dma((heads,)),
                dma((2, heads)), dma((2, heads)),
                dma((2,)), dma((2,)), dma((2, nd - 1)),
            ],
            compiler_params=pltpu.CompilerParams(
                collective_id=0, has_side_effects=True, vmem_limit_bytes=60 * 1024 * 1024
            ),
        )(*(x.reshape(x.shape[2:]) for x in (q, k, v, o, g)), n.reshape(n.shape[2:]).T)
        return tuple(res[i].reshape(lead) for i in range(3))

    return jax.shard_map(
        per_device, mesh=mesh, in_specs=(spec,) * 6, out_specs=(spec,) * 3, check_vma=False
    )
```

```python
import jax
import jax.numpy as jnp
from jax import lax
from jax.experimental import pallas as pl
from jax.experimental.pallas import tpu as pltpu
from jax.sharding import PartitionSpec as P

HD = 128
ROUTES = (((0, 1), (0, 1), (0, 1)), ((0, 1), (0, 1), (0, 1)))
MESH = pl.DeviceIdType.MESH
F32 = jnp.float32
BF16 = jnp.bfloat16
NT = (((1,), (1,)), ((), ()))
NN = (((1,), (0,)), ((), ()))


def dot(a, b, dims):
    return lax.dot_general(a, b, dims, preferred_element_type=F32)


def body(
    nh, nw, nd, heads, tok,
    q_hbm, k_hbm, v_hbm, o_hbm, g_hbm, n_hbm,
    res,
    xin, o_in, n_in, n_out, qd, kv, pad, st_out, st_in, st,
    k_t, dq_acc, kv_acc, rq_send, rq_recv, rk_send, rk_recv, out_send, relay, raw,
    sem_load, s_in, r_in, s_st, r_st, s_z, r_z, s_x, r_x, s_sz, r_sz,
    s_rq, r_rq, s_rk, r_rk, s_out, r_out, s_relay, r_relay, s_raw, r_raw, s_spread,
):
    ih, iw, me = lax.axis_index("ha"), lax.axis_index("wa"), lax.axis_index("hd")
    tile = nd * tok
    scale = HD ** -0.5
    sides_h = (("ha", ih > 0, ih - 1, 0, 2), ("ha", ih < nh - 1, ih + 1, 2, 0))
    sides_w = (("wa", iw > 0, iw - 1, 0, 2), ("wa", iw < nw - 1, iw + 1, 2, 0))
    mid = nw // 2
    vias = (0, 1, 2)
    at_mid = (iw == mid - 1) | (iw == mid)
    detours = lambda r: ((mid - 1, vias[r - 1], mid, 0), (mid, nw - 1 - vias[r - 1], mid - 1, 2))
    met = [(m, v) for m in (mid - 1, mid) for w in vias for v in (w, nw - 1 - w) if abs(m - v) > 1]

    barrier = pltpu.get_barrier_semaphore()

    def greet(t, c):
        pl.semaphore_signal(barrier, inc=1, device_id={"hd": lax.rem(me + 1 + t, nd)}, device_id_type=MESH)
        return c

    lax.fori_loop(0, nd - 1, greet, 0)
    for axis, exists, other, _, _ in sides_h + sides_w:
        @pl.when(exists)
        def _():
            pl.semaphore_signal(barrier, inc=1, device_id={axis: other}, device_id_type=MESH)
    for m, v in met:
        for here, other in ((m, v), (v, m)):
            @pl.when(iw == here)
            def _():
                pl.semaphore_signal(barrier, inc=1, device_id={"wa": other}, device_id_type=MESH)

    loads = [
        pltpu.make_async_copy(src, dst, sem_load.at[n])
        for n, (src, dst) in enumerate((
            (q_hbm, xin.at[0]), (g_hbm, xin.at[1]), (k_hbm, xin.at[2]), (v_hbm, xin.at[3]),
            (o_hbm, o_in), (n_hbm, n_in),
        ))
    ]
    for load in loads:
        load.start()

    for _, exists, _, slot, _ in sides_h:
        @pl.when(jnp.logical_not(exists))
        def _():
            qd[slot] = jnp.zeros(qd.shape[1:], BF16)
            st[slot] = jnp.zeros(st.shape[1:], F32)
            rq_recv[slot // 2] = jnp.zeros(rq_recv.shape[1:], BF16)
    for _, exists, _, slot, _ in sides_w:
        @pl.when(jnp.logical_not(exists))
        def _():
            kv[slot] = jnp.zeros(kv.shape[1:], BF16)
            rk_recv[slot // 2] = jnp.zeros(rk_recv.shape[1:], BF16)

    for load in loads[:4]:
        load.wait()
    count = jnp.int32(nd - 1)
    for _, exists, _, _, _ in sides_h + sides_w:
        count = count + exists.astype(jnp.int32)
    for m, v in met:
        count = count + ((iw == m) | (iw == v)).astype(jnp.int32)
    pl.semaphore_wait(barrier, count)

    def when(side, fn):
        @pl.when(side[1])
        def _():
            fn()

    my_rows = pl.ds(pl.multiple_of(me * tok, tok), tok)

    def spread(h, part, dst):
        def lanes(d):
            return pl.ds(pl.multiple_of((h * nd + d) * HD, HD), HD)

        def one(t, c):
            d = lax.rem(me + 1 + t, nd)
            pltpu.make_async_remote_copy(
                src_ref=xin.at[pl.ds(2 * part, 2), :, lanes(d)],
                dst_ref=dst.at[1, h, :, my_rows, :],
                send_sem=s_in.at[h, part, t], recv_sem=r_in.at[h, part],
                device_id={"hd": d}, device_id_type=MESH,
            ).start()
            return c

        lax.fori_loop(0, nd - 1, one, 0)
        pltpu.make_async_copy(
            xin.at[pl.ds(2 * part, 2), :, lanes(me)], dst.at[1, h, :, my_rows, :], r_in.at[h, part]
        ).start()

    def raw_halo(side):
        axis, _, other, slot, there = side
        return pltpu.make_async_remote_copy(
            src_ref=xin.at[pl.ds(0, 2), :, pl.ds(0, nd * HD)], dst_ref=raw.at[there // 2],
            send_sem=s_raw.at[slot // 2], recv_sem=r_raw.at[there // 2],
            device_id={axis: other}, device_id_type=MESH,
        )

    for side in sides_h:
        when(side, lambda: raw_halo(side).start())
    spread(0, 1, kv)
    spread(1, 0, qd)
    spread(0, 0, qd)

    for load in loads[4:]:
        load.wait()
    lane = lax.broadcasted_iota(jnp.int32, (tok, 128), 1)
    table = jnp.zeros((tok, 128), F32)
    n_out[...] = jnp.zeros(n_out.shape, F32)
    for g in range(nd * heads):
        h, d = g // nd, g % nd
        cols = slice(g * HD, (g + 1) * HD)
        dots = jnp.sum(xin[1, :, cols].astype(F32) * o_in[:, cols].astype(F32), axis=1, keepdims=True)
        n_out[8 * d + h:8 * d + h + 1, :tok] = n_in[g:g + 1, :]
        table = jnp.where(lane == 8 * d + heads + h, dots, table)
    pad[...] = jnp.zeros(pad.shape, F32)
    pad[pl.ds(pl.multiple_of(lax.rem(me, 4) * tok, tok), tok), :] = table
    st_out[...] = pad[...].T[:64] + pltpu.roll(n_out[...], lax.rem(me, 4) * tok, 1)

    def spread_stats(t, c):
        d = lax.rem(me + 1 + t, nd)
        pltpu.make_async_remote_copy(
            src_ref=st_out.at[pl.ds(pl.multiple_of(d * 8, 8), 8), :], dst_ref=st_in.at[me],
            send_sem=s_st.at[t], recv_sem=r_st.at[0], device_id={"hd": d}, device_id_type=MESH,
        ).start()
        return c

    lax.fori_loop(0, nd - 1, spread_stats, 0)
    pltpu.make_async_copy(
        st_out.at[pl.ds(pl.multiple_of(me * 8, 8), 8), :], st_in.at[me], r_st.at[0]
    ).start()

    def halo(buf, h, side, send, recv):
        axis, _, other, slot, there = side
        return pltpu.make_async_remote_copy(
            src_ref=buf.at[1, h], dst_ref=buf.at[there, h],
            send_sem=send.at[h, slot // 2], recv_sem=recv.at[h, there // 2],
            device_id={axis: other}, device_id_type=MESH,
        )

    def seam(side):
        return at_mid & (side[2] == (2 * mid - 1) - iw)

    def leg(src, dst, send, recv, to):
        return pltpu.make_async_remote_copy(
            src_ref=src, dst_ref=dst, send_sem=send, recv_sem=recv,
            device_id={"wa": to}, device_id_type=MESH,
        )

    def send_kv(h, side, src, dst, send, recv, trip):
        @pl.when(side[1] & jnp.logical_not(seam(side)))
        def _():
            leg(src, dst, send, recv, side[2]).start()

        @pl.when(side[1] & seam(side))
        def _():
            for n in range(heads):
                @pl.when(h == n)
                def _():
                    for part, r in enumerate(ROUTES[trip][n]):
                        if r == 0:
                            leg(src.at[part], dst.at[part], send, recv, side[2]).start()
                        else:
                            up, down = detours(r)
                            leg(
                                src.at[part], relay.at[trip, n, part], send, r_relay.at[trip, n, part],
                                jnp.where(iw == mid - 1, up[1], down[1]),
                            ).start()

    def pass_on(h, buf_of, sem_of, trip):
        for part, r in enumerate(ROUTES[trip][h]):
            if r == 0:
                continue
            held = relay.at[trip, h, part]
            for _, via, target, there in detours(r):
                @pl.when(iw == via)
                def _():
                    pltpu.make_async_copy(held, held, r_relay.at[trip, h, part]).wait()
                    leg(held, buf_of(there).at[part], s_relay.at[trip, h, part], sem_of(there), target).start()

    def pass_kv(h):
        pass_on(h, lambda there: kv.at[there, h], lambda there: r_x.at[h, there // 2], 0)

    def pass_back(h):
        pass_on(h, lambda there: rk_recv.at[there // 2, h], lambda there: r_rk.at[there // 2, h], 1)

    def halo_stats(side):
        axis, _, other, slot, there = side
        return pltpu.make_async_remote_copy(
            src_ref=st.at[1], dst_ref=st.at[there],
            send_sem=s_sz.at[slot // 2], recv_sem=r_sz.at[there // 2],
            device_id={axis: other}, device_id_type=MESH,
        )

    def spread_raw(side):
        n = side[3] // 2
        pltpu.make_async_copy(raw.at[n], raw.at[n], r_raw.at[n]).wait()

        def one(t, c):
            d = lax.rem(me + 1 + t, nd)
            pltpu.make_async_remote_copy(
                src_ref=raw.at[n, :, :, pl.ds(pl.multiple_of(d * HD, HD), HD)],
                dst_ref=qd.at[side[3], 0, :, my_rows, :],
                send_sem=s_spread.at[n, t], recv_sem=r_z.at[0, n],
                device_id={"hd": d}, device_id_type=MESH,
            ).start()
            return c

        lax.fori_loop(0, nd - 1, one, 0)
        pltpu.make_async_copy(
            raw.at[n, :, :, pl.ds(pl.multiple_of(me * HD, HD), HD)],
            qd.at[side[3], 0, :, my_rows, :], r_z.at[0, n],
        ).start()

    def own(buf, h, part):
        pltpu.make_async_copy(buf.at[1, h], buf.at[1, h], r_in.at[h, part]).wait()

    def send_rows(h):
        own(qd, h, 0)
        for side in sides_h:
            when(side, lambda: halo(qd, h, side, s_z, r_z).start())

    def send_columns(h):
        own(kv, h, 1)
        for side in sides_w:
            send_kv(h, side, kv.at[1, h], kv.at[side[4], h], s_x.at[h, side[3] // 2], r_x.at[h, side[4] // 2], 0)

    send_columns(0)
    send_rows(1)
    spread(1, 1, kv)
    spread(2, 0, qd)
    pltpu.make_async_copy(st_in, st_in, r_st.at[0]).wait()
    got = st_in[...]
    st[1] = jnp.concatenate(
        [got[0] + got[1] + got[2] + got[3], got[4] + got[5] + got[6] + got[7]], axis=1
    )
    for side in sides_h:
        when(side, lambda: halo_stats(side).start())
    own(qd, 0, 0)
    for side in sides_h:
        when(side, lambda: spread_raw(side))
    spread(2, 1, kv)
    pass_kv(0)
    send_columns(1)
    send_rows(2)
    pass_kv(1)
    send_columns(2)
    pass_kv(2)

    def arrived(buf, slot, h, sem):
        pltpu.make_async_copy(buf.at[slot, h], buf.at[slot, h], sem.at[h, slot // 2]).wait()

    def back_q(h, side):
        axis, _, other, slot, there = side
        return pltpu.make_async_remote_copy(
            src_ref=rq_send.at[slot // 2, h], dst_ref=rq_recv.at[there // 2, h],
            send_sem=s_rq.at[slot // 2, h], recv_sem=r_rq.at[there // 2, h],
            device_id={axis: other}, device_id_type=MESH,
        )

    def back_kv(h, side):
        axis, _, other, slot, there = side
        return pltpu.make_async_remote_copy(
            src_ref=rk_send.at[slot // 2, h], dst_ref=rk_recv.at[there // 2, h],
            send_sem=s_rk.at[slot // 2, h], recv_sem=r_rk.at[there // 2, h],
            device_id={axis: other}, device_id_type=MESH,
        )

    def out_copy(h, t):
        d = lax.rem(me + 1 + t, nd)
        return pltpu.make_async_remote_copy(
            src_ref=out_send.at[h, :, pl.ds(pl.multiple_of(d * tok, tok), tok), :],
            dst_ref=res.at[:, :, pl.ds(pl.multiple_of((h * nd + me) * HD, HD), HD)],
            send_sem=s_out.at[h, t], recv_sem=r_out.at[h],
            device_id={"hd": d}, device_id_type=MESH,
        )

    def compute(h):
        for side in sides_w:
            when(side, lambda: arrived(kv, side[3], h, r_x))
        for b in range(3):
            k_t[b] = kv[b, h, 0].T
        for n, a in enumerate((1, 0, 2)):
            if a != 1:
                side = sides_h[a // 2]
                when(side, lambda: arrived(qd, a, h, r_z))

                @pl.when(side[1] & (h == 0))
                def _():
                    pltpu.make_async_copy(st.at[a], st.at[a], r_sz.at[a // 2]).wait()
            q, g = qd[a, h, 0], qd[a, h, 1]
            norm = st[a, pl.ds(h, 1), :]
            dots = st[a, pl.ds(heads + h, 1), :]
            dq = None
            for b in range(3):
                s_t = dot(kv[b, h, 0], q, NT)
                p_t = jnp.exp(s_t * scale - norm)
                dp_t = dot(kv[b, h, 1], g, NT)
                ds_t = (p_t * (dp_t - dots) * scale).astype(BF16)
                dk = dot(ds_t, q, NN)
                dv = dot(p_t.astype(BF16), g, NN)
                term = dot(k_t[b], ds_t, NN)
                dq = term if dq is None else dq + term
                if n == 0:
                    kv_acc[h, b, 0] = dk
                    kv_acc[h, b, 1] = dv
                else:
                    kv_acc[h, b, 0] += dk
                    kv_acc[h, b, 1] += dv
            if a == 1:
                dq_acc[h] = dq
            else:
                rq_send[a // 2, h] = dq.astype(BF16)
                when(sides_h[a // 2], lambda: back_q(h, sides_h[a // 2]).start())
        for side in sides_w:
            slot = side[3]
            rk_send[slot // 2, h] = kv_acc[h, slot].astype(BF16)
            send_kv(
                h, side, rk_send.at[slot // 2, h], rk_recv.at[side[4] // 2, h],
                s_rk.at[slot // 2, h], r_rk.at[side[4] // 2, h], 1,
            )

    def finish(h):
        for n, side in enumerate(sides_h):
            when(side, lambda: pltpu.make_async_copy(
                rq_recv.at[n, h], rq_recv.at[n, h], r_rq.at[n, h]).wait())
        for n, side in enumerate(sides_w):
            when(side, lambda: pltpu.make_async_copy(
                rk_recv.at[n, h], rk_recv.at[n, h], r_rk.at[n, h]).wait())
        dq = dq_acc[h] + rq_recv[0, h].astype(F32) + rq_recv[1, h].astype(F32)
        out_send[h, 0] = dq.T.astype(BF16)
        for n in range(2):
            out_send[h, 1 + n] = (
                kv_acc[h, 1, n] + rk_recv[0, h, n].astype(F32) + rk_recv[1, h, n].astype(F32)
            ).astype(BF16)

        def one(t, c):
            out_copy(h, t).start()
            return c

        lax.fori_loop(0, nd - 1, one, 0)
        pltpu.make_async_copy(
            out_send.at[h, :, my_rows, :],
            res.at[:, :, pl.ds(pl.multiple_of((h * nd + me) * HD, HD), HD)],
            r_out.at[h],
        ).start()

    def step(h, c):
        compute(h)
        return c

    lax.fori_loop(0, heads, step, 0)
    for h in range(heads - 1):
        pass_back(h)

    def close(h, c):
        finish(h)

        @pl.when(h == 0)
        def _():
            pass_back(heads - 1)
        return c

    lax.fori_loop(0, heads, close, 0)

    def drain(t, c):
        d = lax.rem(me + 1 + t, nd)
        for h in range(heads):
            for part in range(2):
                src = xin.at[pl.ds(2 * part, 2), :, pl.ds(0, HD)]
                pltpu.make_async_copy(src, src, s_in.at[h, part, t]).wait()
            src = out_send.at[h, :, pl.ds(0, tok), :]
            pltpu.make_async_copy(src, src, s_out.at[h, t]).wait()
        src = st_out.at[pl.ds(0, 8), :]
        pltpu.make_async_copy(src, src, s_st.at[t]).wait()
        return c

    lax.fori_loop(0, nd - 1, drain, 0)
    def drain_raw(side):
        def one(t, c):
            src = raw.at[side[3] // 2, :, :, pl.ds(0, HD)]
            pltpu.make_async_copy(src, src, s_spread.at[side[3] // 2, t]).wait()
            return c

        raw_halo(side).wait_send()
        lax.fori_loop(0, nd - 1, one, 0)

    for side in sides_h:
        when(side, lambda: halo_stats(side).wait_send())
        when(side, lambda: drain_raw(side))
    for h in range(heads):
        for side in sides_h:
            if h > 0:
                when(side, lambda: halo(qd, h, side, s_z, r_z).wait_send())
            when(side, lambda: back_q(h, side).wait_send())
        for side in sides_w:
            when(side, lambda: halo(kv, h, side, s_x, r_x).wait_send())
            when(side, lambda: back_kv(h, side).wait_send())

        for trip in range(2):
            for part, r in enumerate(ROUTES[trip][h]):
                if r == 0:
                    continue
                held = relay.at[trip, h, part]
                for _, via, _, _ in detours(r):
                    @pl.when(iw == via)
                    def _():
                        pltpu.make_async_copy(held, held, s_relay.at[trip, h, part]).wait()
    for h in range(heads):
        part = res.at[:, :, pl.ds(0, nd * HD)]
        pltpu.make_async_copy(part, part, r_out.at[h]).wait()


def solution(mesh):
    nh, nw, nd = mesh.shape["ha"], mesh.shape["wa"], mesh.shape["hd"]
    spec = P("ha", "wa", "hd", None)

    def per_device(q, k, v, o, g, n):
        tok, chan = q.shape[2], q.shape[3]
        heads = chan // HD // nd
        tile = tok * nd
        lead = q.shape

        def kernel(*refs):
            body(nh, nw, nd, heads, tok, *refs)

        dma = pltpu.SemaphoreType.DMA
        res = pl.pallas_call(
            kernel,
            out_shape=jax.ShapeDtypeStruct((3, tok, chan), BF16),
            in_specs=[pl.BlockSpec(memory_space=pltpu.HBM)] * 6,
            out_specs=pl.BlockSpec(memory_space=pltpu.HBM),
            scratch_shapes=[
                pltpu.VMEM((4, tok, chan), BF16),
                pltpu.VMEM((tok, chan), BF16),
                pltpu.VMEM((n.shape[3], tok), F32),
                pltpu.VMEM((64, 128), F32),
                pltpu.VMEM((3, heads, 2, tile, HD), BF16),
                pltpu.VMEM((3, heads, 2, tile, HD), BF16),
                pltpu.VMEM((128, 128), F32),
                pltpu.VMEM((64, 128), F32),
                pltpu.VMEM((nd, 8, 128), F32),
                pltpu.VMEM((3, 8, tile), F32),
                pltpu.VMEM((3, HD, tile), BF16),
                pltpu.VMEM((heads, HD, tile), F32),
                pltpu.VMEM((heads, 3, 2, tile, HD), F32),
                pltpu.VMEM((2, heads, HD, tile), BF16),
                pltpu.VMEM((2, heads, HD, tile), BF16),
                pltpu.VMEM((2, heads, 2, tile, HD), BF16),
                pltpu.VMEM((2, heads, 2, tile, HD), BF16),
                pltpu.VMEM((heads, 3, tile, HD), BF16),
                pltpu.VMEM((2, heads, 2, tile, HD), BF16),
                pltpu.VMEM((2, 2, tok, nd * HD), BF16),
                dma((6,)),
                dma((heads, 2, nd - 1)), dma((heads, 2)),
                dma((nd - 1,)), dma((1,)),
                dma((heads, 2)), dma((heads, 2)),
                dma((heads, 2)), dma((heads, 2)),
                dma((2,)), dma((2,)),
                dma((2, heads)), dma((2, heads)),
                dma((2, heads)), dma((2, heads)),
                dma((heads, nd - 1)), dma((heads,)),
                dma((2, heads, 2)), dma((2, heads, 2)),
                dma((2,)), dma((2,)), dma((2, nd - 1)),
            ],
            compiler_params=pltpu.CompilerParams(
                collective_id=0, has_side_effects=True, vmem_limit_bytes=60 * 1024 * 1024
            ),
        )(*(x.reshape(x.shape[2:]) for x in (q, k, v, o, g)), n.reshape(n.shape[2:]).T)
        return tuple(res[i].reshape(lead) for i in range(3))

    return jax.shard_map(
        per_device, mesh=mesh, in_specs=(spec,) * 6, out_specs=(spec,) * 3, check_vma=False
    )
```

```python
import jax
import jax.numpy as jnp
from jax import lax
from jax.experimental import pallas as pl
from jax.experimental.pallas import tpu as pltpu
from jax.sharding import PartitionSpec as P

HD = 128
ROUTES = (((0, 1), (0, 1), (0, 1)), ((0, 1), (0, 1), (0, 1)))
MESH = pl.DeviceIdType.MESH
F32 = jnp.float32
BF16 = jnp.bfloat16
NT = (((1,), (1,)), ((), ()))
NN = (((1,), (0,)), ((), ()))


def dot(a, b, dims):
    return lax.dot_general(a, b, dims, preferred_element_type=F32)


def body(
    nh, nw, nd, heads, tok,
    q_hbm, k_hbm, v_hbm, o_hbm, g_hbm, n_hbm,
    res,
    xin, o_in, n_in, n_out, qd, kv, pad, st_out, st_in, st,
    k_t, dq_acc, kv_acc, rq_send, rq_recv, rk_send, rk_recv, out_send, relay, raw,
    sem_load, s_in, r_in, s_st, r_st, s_z, r_z, s_x, r_x, s_sz, r_sz,
    s_rq, r_rq, s_rk, r_rk, s_out, r_out, s_relay, r_relay, s_raw, r_raw, s_spread,
):
    ih, iw, me = lax.axis_index("ha"), lax.axis_index("wa"), lax.axis_index("hd")
    tile = nd * tok
    scale = HD ** -0.5
    sides_h = (("ha", ih > 0, ih - 1, 0, 2), ("ha", ih < nh - 1, ih + 1, 2, 0))
    sides_w = (("wa", iw > 0, iw - 1, 0, 2), ("wa", iw < nw - 1, iw + 1, 2, 0))
    mid = nw // 2
    vias = (0, 1, 2)
    at_mid = (iw == mid - 1) | (iw == mid)
    detours = lambda r: ((mid - 1, vias[r - 1], mid, 0), (mid, nw - 1 - vias[r - 1], mid - 1, 2))
    met = [(m, v) for m in (mid - 1, mid) for w in vias for v in (w, nw - 1 - w) if abs(m - v) > 1]

    barrier = pltpu.get_barrier_semaphore()

    def greet(t, c):
        pl.semaphore_signal(barrier, inc=1, device_id={"hd": lax.rem(me + 1 + t, nd)}, device_id_type=MESH)
        return c

    lax.fori_loop(0, nd - 1, greet, 0)
    for axis, exists, other, _, _ in sides_h + sides_w:
        @pl.when(exists)
        def _():
            pl.semaphore_signal(barrier, inc=1, device_id={axis: other}, device_id_type=MESH)
    for m, v in met:
        for here, other in ((m, v), (v, m)):
            @pl.when(iw == here)
            def _():
                pl.semaphore_signal(barrier, inc=1, device_id={"wa": other}, device_id_type=MESH)

    loads = [
        pltpu.make_async_copy(src, dst, sem_load.at[n])
        for n, (src, dst) in enumerate((
            (q_hbm, xin.at[0]), (g_hbm, xin.at[1]), (k_hbm, xin.at[2]), (v_hbm, xin.at[3]),
            (o_hbm, o_in), (n_hbm, n_in),
        ))
    ]
    for load in loads:
        load.start()

    for _, exists, _, slot, _ in sides_h:
        @pl.when(jnp.logical_not(exists))
        def _():
            qd[slot] = jnp.zeros(qd.shape[1:], BF16)
            st[slot] = jnp.zeros(st.shape[1:], F32)
            rq_recv[slot // 2] = jnp.zeros(rq_recv.shape[1:], BF16)
    for _, exists, _, slot, _ in sides_w:
        @pl.when(jnp.logical_not(exists))
        def _():
            kv[slot] = jnp.zeros(kv.shape[1:], BF16)
            rk_recv[slot // 2] = jnp.zeros(rk_recv.shape[1:], BF16)

    for load in loads[:4]:
        load.wait()
    count = jnp.int32(nd - 1)
    for _, exists, _, _, _ in sides_h + sides_w:
        count = count + exists.astype(jnp.int32)
    for m, v in met:
        count = count + ((iw == m) | (iw == v)).astype(jnp.int32)
    pl.semaphore_wait(barrier, count)

    def when(side, fn):
        @pl.when(side[1])
        def _():
            fn()

    my_rows = pl.ds(pl.multiple_of(me * tok, tok), tok)

    def spread(h, part, dst):
        def lanes(d):
            return pl.ds(pl.multiple_of((h * nd + d) * HD, HD), HD)

        def one(t, c):
            d = lax.rem(me + 1 + t, nd)
            pltpu.make_async_remote_copy(
                src_ref=xin.at[pl.ds(2 * part, 2), :, lanes(d)],
                dst_ref=dst.at[1, h, :, my_rows, :],
                send_sem=s_in.at[h, part, t], recv_sem=r_in.at[h, part],
                device_id={"hd": d}, device_id_type=MESH,
            ).start()
            return c

        lax.fori_loop(0, nd - 1, one, 0)
        pltpu.make_async_copy(
            xin.at[pl.ds(2 * part, 2), :, lanes(me)], dst.at[1, h, :, my_rows, :], r_in.at[h, part]
        ).start()

    def raw_halo(side):
        axis, _, other, slot, there = side
        return pltpu.make_async_remote_copy(
            src_ref=xin.at[pl.ds(0, 2), :, pl.ds(0, nd * HD)], dst_ref=raw.at[there // 2],
            send_sem=s_raw.at[slot // 2], recv_sem=r_raw.at[there // 2],
            device_id={axis: other}, device_id_type=MESH,
        )

    for side in sides_h:
        when(side, lambda: raw_halo(side).start())
    spread(0, 1, kv)
    spread(1, 0, qd)
    spread(0, 0, qd)

    for load in loads[4:]:
        load.wait()
    lane = lax.broadcasted_iota(jnp.int32, (tok, 128), 1)
    table = jnp.zeros((tok, 128), F32)
    n_out[...] = jnp.zeros(n_out.shape, F32)
    for g in range(nd * heads):
        h, d = g // nd, g % nd
        cols = slice(g * HD, (g + 1) * HD)
        dots = jnp.sum(xin[1, :, cols].astype(F32) * o_in[:, cols].astype(F32), axis=1, keepdims=True)
        n_out[8 * d + h:8 * d + h + 1, :tok] = n_in[g:g + 1, :]
        table = jnp.where(lane == 8 * d + heads + h, dots, table)
    pad[...] = jnp.zeros(pad.shape, F32)
    pad[pl.ds(pl.multiple_of(lax.rem(me, 4) * tok, tok), tok), :] = table
    st_out[...] = pad[...].T[:64] + pltpu.roll(n_out[...], lax.rem(me, 4) * tok, 1)

    def spread_stats(t, c):
        d = lax.rem(me + 1 + t, nd)
        pltpu.make_async_remote_copy(
            src_ref=st_out.at[pl.ds(pl.multiple_of(d * 8, 8), 8), :], dst_ref=st_in.at[me],
            send_sem=s_st.at[t], recv_sem=r_st.at[0], device_id={"hd": d}, device_id_type=MESH,
        ).start()
        return c

    lax.fori_loop(0, nd - 1, spread_stats, 0)
    pltpu.make_async_copy(
        st_out.at[pl.ds(pl.multiple_of(me * 8, 8), 8), :], st_in.at[me], r_st.at[0]
    ).start()

    def halo(buf, h, side, send, recv):
        axis, _, other, slot, there = side
        return pltpu.make_async_remote_copy(
            src_ref=buf.at[1, h], dst_ref=buf.at[there, h],
            send_sem=send.at[h, slot // 2], recv_sem=recv.at[h, there // 2],
            device_id={axis: other}, device_id_type=MESH,
        )

    def seam(side):
        return at_mid & (side[2] == (2 * mid - 1) - iw)

    def leg(src, dst, send, recv, to):
        return pltpu.make_async_remote_copy(
            src_ref=src, dst_ref=dst, send_sem=send, recv_sem=recv,
            device_id={"wa": to}, device_id_type=MESH,
        )

    def send_kv(h, side, src, dst, send, recv, trip):
        @pl.when(side[1] & jnp.logical_not(seam(side)))
        def _():
            leg(src, dst, send, recv, side[2]).start()

        @pl.when(side[1] & seam(side))
        def _():
            for n in range(heads):
                @pl.when(h == n)
                def _():
                    for part, r in enumerate(ROUTES[trip][n]):
                        if r == 0:
                            leg(src.at[part], dst.at[part], send, recv, side[2]).start()
                        else:
                            up, down = detours(r)
                            leg(
                                src.at[part], relay.at[trip, n, part], send, r_relay.at[trip, n, part],
                                jnp.where(iw == mid - 1, up[1], down[1]),
                            ).start()

    def pass_on(h, buf_of, sem_of, trip):
        for part, r in enumerate(ROUTES[trip][h]):
            if r == 0:
                continue
            held = relay.at[trip, h, part]
            for _, via, target, there in detours(r):
                @pl.when(iw == via)
                def _():
                    pltpu.make_async_copy(held, held, r_relay.at[trip, h, part]).wait()
                    leg(held, buf_of(there).at[part], s_relay.at[trip, h, part], sem_of(there), target).start()

    def pass_kv(h):
        pass_on(h, lambda there: kv.at[there, h], lambda there: r_x.at[h, there // 2], 0)

    def pass_back(h):
        pass_on(h, lambda there: rk_recv.at[there // 2, h], lambda there: r_rk.at[there // 2, h], 1)

    def halo_stats(side):
        axis, _, other, slot, there = side
        return pltpu.make_async_remote_copy(
            src_ref=st.at[1], dst_ref=st.at[there],
            send_sem=s_sz.at[slot // 2], recv_sem=r_sz.at[there // 2],
            device_id={axis: other}, device_id_type=MESH,
        )

    def spread_raw(side):
        n = side[3] // 2
        pltpu.make_async_copy(raw.at[n], raw.at[n], r_raw.at[n]).wait()

        def one(t, c):
            d = lax.rem(me + 1 + t, nd)
            pltpu.make_async_remote_copy(
                src_ref=raw.at[n, :, :, pl.ds(pl.multiple_of(d * HD, HD), HD)],
                dst_ref=qd.at[side[3], 0, :, my_rows, :],
                send_sem=s_spread.at[n, t], recv_sem=r_z.at[0, n],
                device_id={"hd": d}, device_id_type=MESH,
            ).start()
            return c

        lax.fori_loop(0, nd - 1, one, 0)
        pltpu.make_async_copy(
            raw.at[n, :, :, pl.ds(pl.multiple_of(me * HD, HD), HD)],
            qd.at[side[3], 0, :, my_rows, :], r_z.at[0, n],
        ).start()

    def own(buf, h, part):
        pltpu.make_async_copy(buf.at[1, h], buf.at[1, h], r_in.at[h, part]).wait()

    def send_rows(h):
        own(qd, h, 0)
        for side in sides_h:
            when(side, lambda: halo(qd, h, side, s_z, r_z).start())

    def send_columns(h):
        own(kv, h, 1)
        for side in sides_w:
            send_kv(h, side, kv.at[1, h], kv.at[side[4], h], s_x.at[h, side[3] // 2], r_x.at[h, side[4] // 2], 0)

    send_columns(0)
    send_rows(1)
    spread(1, 1, kv)
    spread(2, 0, qd)
    pltpu.make_async_copy(st_in, st_in, r_st.at[0]).wait()
    got = st_in[...]
    st[1] = jnp.concatenate(
        [got[0] + got[1] + got[2] + got[3], got[4] + got[5] + got[6] + got[7]], axis=1
    )
    for side in sides_h:
        when(side, lambda: halo_stats(side).start())
    own(qd, 0, 0)
    for side in sides_h:
        when(side, lambda: spread_raw(side))
    spread(2, 1, kv)
    pass_kv(0)
    send_columns(1)
    send_rows(2)
    pass_kv(1)
    send_columns(2)
    pass_kv(2)

    def arrived(buf, slot, h, sem):
        pltpu.make_async_copy(buf.at[slot, h], buf.at[slot, h], sem.at[h, slot // 2]).wait()

    def back_q(h, side):
        axis, _, other, slot, there = side
        return pltpu.make_async_remote_copy(
            src_ref=rq_send.at[slot // 2, h], dst_ref=rq_recv.at[there // 2, h],
            send_sem=s_rq.at[slot // 2, h], recv_sem=r_rq.at[there // 2, h],
            device_id={axis: other}, device_id_type=MESH,
        )

    def back_kv(h, side):
        axis, _, other, slot, there = side
        return pltpu.make_async_remote_copy(
            src_ref=rk_send.at[slot // 2, h], dst_ref=rk_recv.at[there // 2, h],
            send_sem=s_rk.at[slot // 2, h], recv_sem=r_rk.at[there // 2, h],
            device_id={axis: other}, device_id_type=MESH,
        )

    def out_copy(h, t):
        d = lax.rem(me + 1 + t, nd)
        return pltpu.make_async_remote_copy(
            src_ref=out_send.at[h, :, pl.ds(pl.multiple_of(d * tok, tok), tok), :],
            dst_ref=res.at[:, :, pl.ds(pl.multiple_of((h * nd + me) * HD, HD), HD)],
            send_sem=s_out.at[h, t], recv_sem=r_out.at[h],
            device_id={"hd": d}, device_id_type=MESH,
        )

    def compute(h):
        for side in sides_w:
            when(side, lambda: arrived(kv, side[3], h, r_x))
        for b in range(3):
            k_t[b] = kv[b, h, 0].T
        for n, a in enumerate((1, 0, 2)):
            if a != 1:
                side = sides_h[a // 2]
                when(side, lambda: arrived(qd, a, h, r_z))

                @pl.when(side[1] & (h == 0))
                def _():
                    pltpu.make_async_copy(st.at[a], st.at[a], r_sz.at[a // 2]).wait()
            q, g = qd[a, h, 0], qd[a, h, 1]
            norm = st[a, pl.ds(h, 1), :]
            dots = st[a, pl.ds(heads + h, 1), :]
            dq = None
            for b in range(3):
                s_t = dot(kv[b, h, 0], q, NT)
                p_t = jnp.exp(s_t * scale - norm)
                dp_t = dot(kv[b, h, 1], g, NT)
                ds_t = (p_t * (dp_t - dots) * scale).astype(BF16)
                dk = dot(ds_t, q, NN)
                dv = dot(p_t.astype(BF16), g, NN)
                term = dot(k_t[b], ds_t, NN)
                dq = term if dq is None else dq + term
                if n == 0:
                    kv_acc[h, b, 0] = dk
                    kv_acc[h, b, 1] = dv
                else:
                    kv_acc[h, b, 0] += dk
                    kv_acc[h, b, 1] += dv
            if a == 1:
                dq_acc[h] = dq
            else:
                rq_send[a // 2, h] = dq.astype(BF16)
                when(sides_h[a // 2], lambda: back_q(h, sides_h[a // 2]).start())
        for side in sides_w:
            slot = side[3]
            rk_send[slot // 2, h] = kv_acc[h, slot].astype(BF16)
            send_kv(
                h, side, rk_send.at[slot // 2, h], rk_recv.at[side[4] // 2, h],
                s_rk.at[slot // 2, h], r_rk.at[side[4] // 2, h], 1,
            )

    def finish(h):
        for n, side in enumerate(sides_h):
            when(side, lambda: pltpu.make_async_copy(
                rq_recv.at[n, h], rq_recv.at[n, h], r_rq.at[n, h]).wait())
        for n, side in enumerate(sides_w):
            when(side, lambda: pltpu.make_async_copy(
                rk_recv.at[n, h], rk_recv.at[n, h], r_rk.at[n, h]).wait())
        dq = dq_acc[h] + rq_recv[0, h].astype(F32) + rq_recv[1, h].astype(F32)
        out_send[h, 0] = dq.T.astype(BF16)
        for n in range(2):
            out_send[h, 1 + n] = (
                kv_acc[h, 1, n] + rk_recv[0, h, n].astype(F32) + rk_recv[1, h, n].astype(F32)
            ).astype(BF16)

        def one(t, c):
            out_copy(h, t).start()
            return c

        lax.fori_loop(0, nd - 1, one, 0)
        pltpu.make_async_copy(
            out_send.at[h, :, my_rows, :],
            res.at[:, :, pl.ds(pl.multiple_of((h * nd + me) * HD, HD), HD)],
            r_out.at[h],
        ).start()

    def step(h, c):
        compute(h)
        return c

    lax.fori_loop(0, heads, step, 0)
    for h in range(heads - 1):
        pass_back(h)

    def close(h, c):
        finish(h)

        @pl.when(h == 0)
        def _():
            pass_back(heads - 1)
        return c

    lax.fori_loop(0, heads, close, 0)

    def drain(t, c):
        d = lax.rem(me + 1 + t, nd)
        for h in range(heads):
            for part in range(2):
                src = xin.at[pl.ds(2 * part, 2), :, pl.ds(0, HD)]
                pltpu.make_async_copy(src, src, s_in.at[h, part, t]).wait()
            src = out_send.at[h, :, pl.ds(0, tok), :]
            pltpu.make_async_copy(src, src, s_out.at[h, t]).wait()
        src = st_out.at[pl.ds(0, 8), :]
        pltpu.make_async_copy(src, src, s_st.at[t]).wait()
        return c

    lax.fori_loop(0, nd - 1, drain, 0)
    def drain_raw(side):
        def one(t, c):
            src = raw.at[side[3] // 2, :, :, pl.ds(0, HD)]
            pltpu.make_async_copy(src, src, s_spread.at[side[3] // 2, t]).wait()
            return c

        raw_halo(side).wait_send()
        lax.fori_loop(0, nd - 1, one, 0)

    for side in sides_h:
        when(side, lambda: halo_stats(side).wait_send())
        when(side, lambda: drain_raw(side))
    for h in range(heads):
        for side in sides_h:
            if h > 0:
                when(side, lambda: halo(qd, h, side, s_z, r_z).wait_send())
            when(side, lambda: back_q(h, side).wait_send())
        for side in sides_w:
            when(side, lambda: halo(kv, h, side, s_x, r_x).wait_send())
            when(side, lambda: back_kv(h, side).wait_send())

        for trip in range(2):
            for part, r in enumerate(ROUTES[trip][h]):
                if r == 0:
                    continue
                held = relay.at[trip, h, part]
                for _, via, _, _ in detours(r):
                    @pl.when(iw == via)
                    def _():
                        pltpu.make_async_copy(held, held, s_relay.at[trip, h, part]).wait()
    for h in range(heads):
        part = res.at[:, :, pl.ds(0, nd * HD)]
        pltpu.make_async_copy(part, part, r_out.at[h]).wait()


def solution(mesh):
    nh, nw, nd = mesh.shape["ha"], mesh.shape["wa"], mesh.shape["hd"]
    spec = P("ha", "wa", "hd", None)

    def per_device(q, k, v, o, g, n):
        tok, chan = q.shape[2], q.shape[3]
        heads = chan // HD // nd
        tile = tok * nd
        lead = q.shape

        def kernel(*refs):
            body(nh, nw, nd, heads, tok, *refs)

        dma = pltpu.SemaphoreType.DMA
        res = pl.pallas_call(
            kernel,
            out_shape=pltpu.VMEM((3, tok, chan), BF16),
            in_specs=[pl.BlockSpec(memory_space=pltpu.HBM)] * 6,
            out_specs=pl.BlockSpec(memory_space=pltpu.VMEM),
            scratch_shapes=[
                pltpu.VMEM((4, tok, chan), BF16),
                pltpu.VMEM((tok, chan), BF16),
                pltpu.VMEM((n.shape[3], tok), F32),
                pltpu.VMEM((64, 128), F32),
                pltpu.VMEM((3, heads, 2, tile, HD), BF16),
                pltpu.VMEM((3, heads, 2, tile, HD), BF16),
                pltpu.VMEM((128, 128), F32),
                pltpu.VMEM((64, 128), F32),
                pltpu.VMEM((nd, 8, 128), F32),
                pltpu.VMEM((3, 8, tile), F32),
                pltpu.VMEM((3, HD, tile), BF16),
                pltpu.VMEM((heads, HD, tile), F32),
                pltpu.VMEM((heads, 3, 2, tile, HD), F32),
                pltpu.VMEM((2, heads, HD, tile), BF16),
                pltpu.VMEM((2, heads, HD, tile), BF16),
                pltpu.VMEM((2, heads, 2, tile, HD), BF16),
                pltpu.VMEM((2, heads, 2, tile, HD), BF16),
                pltpu.VMEM((heads, 3, tile, HD), BF16),
                pltpu.VMEM((2, heads, 2, tile, HD), BF16),
                pltpu.VMEM((2, 2, tok, nd * HD), BF16),
                dma((6,)),
                dma((heads, 2, nd - 1)), dma((heads, 2)),
                dma((nd - 1,)), dma((1,)),
                dma((heads, 2)), dma((heads, 2)),
                dma((heads, 2)), dma((heads, 2)),
                dma((2,)), dma((2,)),
                dma((2, heads)), dma((2, heads)),
                dma((2, heads)), dma((2, heads)),
                dma((heads, nd - 1)), dma((heads,)),
                dma((2, heads, 2)), dma((2, heads, 2)),
                dma((2,)), dma((2,)), dma((2, nd - 1)),
            ],
            compiler_params=pltpu.CompilerParams(
                collective_id=0, has_side_effects=True, vmem_limit_bytes=60 * 1024 * 1024
            ),
        )(*(x.reshape(x.shape[2:]) for x in (q, k, v, o, g)), n.reshape(n.shape[2:]).T)
        return tuple(res[i].reshape(lead) for i in range(3))

    return jax.shard_map(
        per_device, mesh=mesh, in_specs=(spec,) * 6, out_specs=(spec,) * 3, check_vma=False
    )
```

```python
import jax
import jax.numpy as jnp
from jax import lax
from jax.experimental import pallas as pl
from jax.experimental.pallas import tpu as pltpu
from jax.sharding import PartitionSpec as P

HD = 128
ROUTES = (((0, 1), (0, 1), (0, 1)), ((0, 1), (0, 1), (0, 0)))
MESH = pl.DeviceIdType.MESH
F32 = jnp.float32
BF16 = jnp.bfloat16
NT = (((1,), (1,)), ((), ()))
NN = (((1,), (0,)), ((), ()))


def dot(a, b, dims):
    return lax.dot_general(a, b, dims, preferred_element_type=F32)


def body(
    nh, nw, nd, heads, tok,
    q_hbm, k_hbm, v_hbm, o_hbm, g_hbm, n_hbm,
    res,
    xin, o_in, n_in, n_out, qd, kv, pad, st_out, st_in, st,
    k_t, dq_acc, kv_acc, rq_send, rq_recv, rk_send, rk_recv, out_send, relay, raw,
    sem_load, s_in, r_in, s_st, r_st, s_z, r_z, s_x, r_x, s_sz, r_sz,
    s_rq, r_rq, s_rk, r_rk, s_out, s_out2, r_out, s_relay, r_relay, s_raw, r_raw, s_spread,
):
    ih, iw, me = lax.axis_index("ha"), lax.axis_index("wa"), lax.axis_index("hd")
    tile = nd * tok
    scale = HD ** -0.5
    sides_h = (("ha", ih > 0, ih - 1, 0, 2), ("ha", ih < nh - 1, ih + 1, 2, 0))
    sides_w = (("wa", iw > 0, iw - 1, 0, 2), ("wa", iw < nw - 1, iw + 1, 2, 0))
    mid = nw // 2
    vias = (0, 1, 2)
    at_mid = (iw == mid - 1) | (iw == mid)
    detours = lambda r: ((mid - 1, vias[r - 1], mid, 0), (mid, nw - 1 - vias[r - 1], mid - 1, 2))
    met = [(m, v) for m in (mid - 1, mid) for w in vias for v in (w, nw - 1 - w) if abs(m - v) > 1]

    barrier = pltpu.get_barrier_semaphore()

    def greet(t, c):
        pl.semaphore_signal(barrier, inc=1, device_id={"hd": lax.rem(me + 1 + t, nd)}, device_id_type=MESH)
        return c

    lax.fori_loop(0, nd - 1, greet, 0)
    for axis, exists, other, _, _ in sides_h + sides_w:
        @pl.when(exists)
        def _():
            pl.semaphore_signal(barrier, inc=1, device_id={axis: other}, device_id_type=MESH)
    for m, v in met:
        for here, other in ((m, v), (v, m)):
            @pl.when(iw == here)
            def _():
                pl.semaphore_signal(barrier, inc=1, device_id={"wa": other}, device_id_type=MESH)

    loads = [
        pltpu.make_async_copy(src, dst, sem_load.at[n])
        for n, (src, dst) in enumerate((
            (q_hbm, xin.at[0]), (g_hbm, xin.at[1]), (k_hbm, xin.at[2]), (v_hbm, xin.at[3]),
            (o_hbm, o_in), (n_hbm, n_in),
        ))
    ]
    for load in loads:
        load.start()

    for _, exists, _, slot, _ in sides_h:
        @pl.when(jnp.logical_not(exists))
        def _():
            qd[slot] = jnp.zeros(qd.shape[1:], BF16)
            st[slot] = jnp.zeros(st.shape[1:], F32)
            rq_recv[slot // 2] = jnp.zeros(rq_recv.shape[1:], BF16)
    for _, exists, _, slot, _ in sides_w:
        @pl.when(jnp.logical_not(exists))
        def _():
            kv[slot] = jnp.zeros(kv.shape[1:], BF16)
            rk_recv[slot // 2] = jnp.zeros(rk_recv.shape[1:], BF16)

    for load in loads[:4]:
        load.wait()
    count = jnp.int32(nd - 1)
    for _, exists, _, _, _ in sides_h + sides_w:
        count = count + exists.astype(jnp.int32)
    for m, v in met:
        count = count + ((iw == m) | (iw == v)).astype(jnp.int32)
    pl.semaphore_wait(barrier, count)

    def when(side, fn):
        @pl.when(side[1])
        def _():
            fn()

    my_rows = pl.ds(pl.multiple_of(me * tok, tok), tok)

    def spread(h, part, dst):
        def lanes(d):
            return pl.ds(pl.multiple_of((h * nd + d) * HD, HD), HD)

        def one(t, c):
            d = lax.rem(me + 1 + t, nd)
            pltpu.make_async_remote_copy(
                src_ref=xin.at[pl.ds(2 * part, 2), :, lanes(d)],
                dst_ref=dst.at[1, h, :, my_rows, :],
                send_sem=s_in.at[h, part, t], recv_sem=r_in.at[h, part],
                device_id={"hd": d}, device_id_type=MESH,
            ).start()
            return c

        lax.fori_loop(0, nd - 1, one, 0)
        pltpu.make_async_copy(
            xin.at[pl.ds(2 * part, 2), :, lanes(me)], dst.at[1, h, :, my_rows, :], r_in.at[h, part]
        ).start()

    def raw_halo(side):
        axis, _, other, slot, there = side
        return pltpu.make_async_remote_copy(
            src_ref=xin.at[pl.ds(0, 2), :, pl.ds(0, nd * HD)], dst_ref=raw.at[there // 2],
            send_sem=s_raw.at[slot // 2], recv_sem=r_raw.at[there // 2],
            device_id={axis: other}, device_id_type=MESH,
        )

    for side in sides_h:
        when(side, lambda: raw_halo(side).start())
    spread(0, 1, kv)
    spread(1, 0, qd)
    spread(0, 0, qd)

    for load in loads[4:]:
        load.wait()
    lane = lax.broadcasted_iota(jnp.int32, (tok, 128), 1)
    table = jnp.zeros((tok, 128), F32)
    n_out[...] = jnp.zeros(n_out.shape, F32)
    for g in range(nd * heads):
        h, d = g // nd, g % nd
        cols = slice(g * HD, (g + 1) * HD)
        dots = jnp.sum(xin[1, :, cols].astype(F32) * o_in[:, cols].astype(F32), axis=1, keepdims=True)
        n_out[8 * d + h:8 * d + h + 1, :tok] = n_in[g:g + 1, :]
        table = jnp.where(lane == 8 * d + heads + h, dots, table)
    pad[...] = jnp.zeros(pad.shape, F32)
    pad[pl.ds(pl.multiple_of(lax.rem(me, 4) * tok, tok), tok), :] = table
    st_out[...] = pad[...].T[:64] + pltpu.roll(n_out[...], lax.rem(me, 4) * tok, 1)

    def spread_stats(t, c):
        d = lax.rem(me + 1 + t, nd)
        pltpu.make_async_remote_copy(
            src_ref=st_out.at[pl.ds(pl.multiple_of(d * 8, 8), 8), :], dst_ref=st_in.at[me],
            send_sem=s_st.at[t], recv_sem=r_st.at[0], device_id={"hd": d}, device_id_type=MESH,
        ).start()
        return c

    lax.fori_loop(0, nd - 1, spread_stats, 0)
    pltpu.make_async_copy(
        st_out.at[pl.ds(pl.multiple_of(me * 8, 8), 8), :], st_in.at[me], r_st.at[0]
    ).start()

    def halo(buf, h, side, send, recv):
        axis, _, other, slot, there = side
        return pltpu.make_async_remote_copy(
            src_ref=buf.at[1, h], dst_ref=buf.at[there, h],
            send_sem=send.at[h, slot // 2], recv_sem=recv.at[h, there // 2],
            device_id={axis: other}, device_id_type=MESH,
        )

    def seam(side):
        return at_mid & (side[2] == (2 * mid - 1) - iw)

    def leg(src, dst, send, recv, to):
        return pltpu.make_async_remote_copy(
            src_ref=src, dst_ref=dst, send_sem=send, recv_sem=recv,
            device_id={"wa": to}, device_id_type=MESH,
        )

    def send_kv(h, side, src, dst, send, recv, trip):
        @pl.when(side[1] & jnp.logical_not(seam(side)))
        def _():
            leg(src, dst, send, recv, side[2]).start()

        @pl.when(side[1] & seam(side))
        def _():
            for n in range(heads):
                @pl.when(h == n)
                def _():
                    for part, r in enumerate(ROUTES[trip][n]):
                        if r == 0:
                            leg(src.at[part], dst.at[part], send, recv, side[2]).start()
                        else:
                            up, down = detours(r)
                            leg(
                                src.at[part], relay.at[trip, n, part], send, r_relay.at[trip, n, part],
                                jnp.where(iw == mid - 1, up[1], down[1]),
                            ).start()

    def pass_on(h, buf_of, sem_of, trip):
        for part, r in enumerate(ROUTES[trip][h]):
            if r == 0:
                continue
            held = relay.at[trip, h, part]
            for _, via, target, there in detours(r):
                @pl.when(iw == via)
                def _():
                    pltpu.make_async_copy(held, held, r_relay.at[trip, h, part]).wait()
                    leg(held, buf_of(there).at[part], s_relay.at[trip, h, part], sem_of(there), target).start()

    def pass_kv(h):
        pass_on(h, lambda there: kv.at[there, h], lambda there: r_x.at[h, there // 2], 0)

    def pass_back(h):
        pass_on(h, lambda there: rk_recv.at[there // 2, h], lambda there: r_rk.at[there // 2, h], 1)

    def halo_stats(side):
        axis, _, other, slot, there = side
        return pltpu.make_async_remote_copy(
            src_ref=st.at[1], dst_ref=st.at[there],
            send_sem=s_sz.at[slot // 2], recv_sem=r_sz.at[there // 2],
            device_id={axis: other}, device_id_type=MESH,
        )

    def spread_raw(side):
        n = side[3] // 2
        pltpu.make_async_copy(raw.at[n], raw.at[n], r_raw.at[n]).wait()

        def one(t, c):
            d = lax.rem(me + 1 + t, nd)
            pltpu.make_async_remote_copy(
                src_ref=raw.at[n, :, :, pl.ds(pl.multiple_of(d * HD, HD), HD)],
                dst_ref=qd.at[side[3], 0, :, my_rows, :],
                send_sem=s_spread.at[n, t], recv_sem=r_z.at[0, n],
                device_id={"hd": d}, device_id_type=MESH,
            ).start()
            return c

        lax.fori_loop(0, nd - 1, one, 0)
        pltpu.make_async_copy(
            raw.at[n, :, :, pl.ds(pl.multiple_of(me * HD, HD), HD)],
            qd.at[side[3], 0, :, my_rows, :], r_z.at[0, n],
        ).start()

    def own(buf, h, part):
        pltpu.make_async_copy(buf.at[1, h], buf.at[1, h], r_in.at[h, part]).wait()

    def send_rows(h):
        own(qd, h, 0)
        for side in sides_h:
            when(side, lambda: halo(qd, h, side, s_z, r_z).start())

    def send_columns(h):
        own(kv, h, 1)
        for side in sides_w:
            send_kv(h, side, kv.at[1, h], kv.at[side[4], h], s_x.at[h, side[3] // 2], r_x.at[h, side[4] // 2], 0)

    send_columns(0)
    send_rows(1)
    spread(1, 1, kv)
    spread(2, 0, qd)
    pltpu.make_async_copy(st_in, st_in, r_st.at[0]).wait()
    got = st_in[...]
    st[1] = jnp.concatenate(
        [got[0] + got[1] + got[2] + got[3], got[4] + got[5] + got[6] + got[7]], axis=1
    )
    for side in sides_h:
        when(side, lambda: halo_stats(side).start())
    own(qd, 0, 0)
    for side in sides_h:
        when(side, lambda: spread_raw(side))
    spread(2, 1, kv)
    pass_kv(0)
    send_columns(1)
    send_rows(2)
    pass_kv(1)
    send_columns(2)
    pass_kv(2)

    def arrived(buf, slot, h, sem):
        pltpu.make_async_copy(buf.at[slot, h], buf.at[slot, h], sem.at[h, slot // 2]).wait()

    def back_q(h, side):
        axis, _, other, slot, there = side
        return pltpu.make_async_remote_copy(
            src_ref=rq_send.at[slot // 2, h], dst_ref=rq_recv.at[there // 2, h],
            send_sem=s_rq.at[slot // 2, h], recv_sem=r_rq.at[there // 2, h],
            device_id={axis: other}, device_id_type=MESH,
        )

    def back_kv(h, side):
        axis, _, other, slot, there = side
        return pltpu.make_async_remote_copy(
            src_ref=rk_send.at[slot // 2, h], dst_ref=rk_recv.at[there // 2, h],
            send_sem=s_rk.at[slot // 2, h], recv_sem=r_rk.at[there // 2, h],
            device_id={axis: other}, device_id_type=MESH,
        )

    first_b = jnp.where(iw == mid, 2, 0)
    last_b = 2 - first_b

    def wait_columns(h, b):
        for side in sides_w:
            @pl.when(side[1] & (b == side[3]))
            def _():
                arrived(kv, side[3], h, r_x)

    def compute(h):
        def pair(a, b, new_q, new_kv):
            q, g = qd[a, h, 0], qd[a, h, 1]
            norm = st[a, pl.ds(h, 1), :]
            dots = st[a, pl.ds(heads + h, 1), :]
            s_t = dot(kv[b, h, 0], q, NT)
            p_t = jnp.exp(s_t * scale - norm)
            dp_t = dot(kv[b, h, 1], g, NT)
            ds_t = (p_t * (dp_t - dots) * scale).astype(BF16)
            dk = dot(ds_t, q, NN)
            dv = dot(p_t.astype(BF16), g, NN)
            dq = dot(k_t[b], ds_t, NN)
            if new_q:
                dq_acc[h, a] = dq
            else:
                dq_acc[h, a] += dq
            if new_kv:
                kv_acc[h, b, 0] = dk
                kv_acc[h, b, 1] = dv
            else:
                kv_acc[h, b, 0] += dk
                kv_acc[h, b, 1] += dv

        def back_columns(b):
            for side in sides_w:
                slot = side[3]

                @pl.when(b == slot)
                def _():
                    rk_send[slot // 2, h] = kv_acc[h, slot].astype(BF16)
                    send_kv(
                        h, side, rk_send.at[slot // 2, h], rk_recv.at[side[4] // 2, h],
                        s_rk.at[slot // 2, h], r_rk.at[side[4] // 2, h], 1,
                    )

        def back_rows(a):
            rq_send[a // 2, h] = dq_acc[h, a].astype(BF16)
            when(sides_h[a // 2], lambda: back_q(h, sides_h[a // 2]).start())

        k_t[1] = kv[1, h, 0].T
        pair(1, 1, True, True)
        wait_columns(h, first_b)
        k_t[first_b] = kv[first_b, h, 0].T
        pair(1, first_b, False, True)
        for side in sides_h:
            when(side, lambda: arrived(qd, side[3], h, r_z))

            @pl.when(side[1] & (h == 0))
            def _():
                pltpu.make_async_copy(st.at[side[3]], st.at[side[3]], r_sz.at[side[3] // 2]).wait()
        pair(0, first_b, True, False)
        pair(2, first_b, True, False)
        back_columns(first_b)
        pair(0, 1, False, False)
        pair(2, 1, False, False)
        wait_columns(h, last_b)
        k_t[last_b] = kv[last_b, h, 0].T
        pair(0, last_b, False, True)
        back_rows(0)
        pair(2, last_b, False, False)
        back_rows(2)
        pair(1, last_b, False, False)
        back_columns(last_b)

    def out_copy(h, t, rows, sem):
        d = lax.rem(me + 1 + t, nd)
        return pltpu.make_async_remote_copy(
            src_ref=out_send.at[h, rows, pl.ds(pl.multiple_of(d * tok, tok), tok), :],
            dst_ref=res.at[rows, :, pl.ds(pl.multiple_of((h * nd + me) * HD, HD), HD)],
            send_sem=sem.at[h, t], recv_sem=r_out.at[h],
            device_id={"hd": d}, device_id_type=MESH,
        )

    def send_out(h, rows, sem):
        def one(t, c):
            out_copy(h, t, rows, sem).start()
            return c

        lax.fori_loop(0, nd - 1, one, 0)
        pltpu.make_async_copy(
            out_send.at[h, rows, my_rows, :],
            res.at[rows, :, pl.ds(pl.multiple_of((h * nd + me) * HD, HD), HD)],
            r_out.at[h],
        ).start()

    def finish(h):
        for n, side in enumerate(sides_h):
            when(side, lambda: pltpu.make_async_copy(
                rq_recv.at[n, h], rq_recv.at[n, h], r_rq.at[n, h]).wait())
        dq = dq_acc[h, 1] + rq_recv[0, h].astype(F32) + rq_recv[1, h].astype(F32)
        out_send[h, 0] = dq.T.astype(BF16)
        send_out(h, pl.ds(0, 1), s_out)
        for n, side in enumerate(sides_w):
            when(side, lambda: pltpu.make_async_copy(
                rk_recv.at[n, h], rk_recv.at[n, h], r_rk.at[n, h]).wait())
        for n in range(2):
            out_send[h, 1 + n] = (
                kv_acc[h, 1, n] + rk_recv[0, h, n].astype(F32) + rk_recv[1, h, n].astype(F32)
            ).astype(BF16)
        send_out(h, pl.ds(1, 2), s_out2)

    def step(h, c):
        compute(h)
        return c

    lax.fori_loop(0, heads, step, 0)
    for h in range(heads - 1):
        pass_back(h)

    def close(h, c):
        finish(h)

        @pl.when(h == 0)
        def _():
            pass_back(heads - 1)
        return c

    lax.fori_loop(0, heads, close, 0)

    def drain(t, c):
        d = lax.rem(me + 1 + t, nd)
        for h in range(heads):
            for part in range(2):
                src = xin.at[pl.ds(2 * part, 2), :, pl.ds(0, HD)]
                pltpu.make_async_copy(src, src, s_in.at[h, part, t]).wait()
            for rows, sem in ((pl.ds(0, 1), s_out), (pl.ds(1, 2), s_out2)):
                src = out_send.at[h, rows, pl.ds(0, tok), :]
                pltpu.make_async_copy(src, src, sem.at[h, t]).wait()
        src = st_out.at[pl.ds(0, 8), :]
        pltpu.make_async_copy(src, src, s_st.at[t]).wait()
        return c

    lax.fori_loop(0, nd - 1, drain, 0)
    def drain_raw(side):
        def one(t, c):
            src = raw.at[side[3] // 2, :, :, pl.ds(0, HD)]
            pltpu.make_async_copy(src, src, s_spread.at[side[3] // 2, t]).wait()
            return c

        raw_halo(side).wait_send()
        lax.fori_loop(0, nd - 1, one, 0)

    for side in sides_h:
        when(side, lambda: halo_stats(side).wait_send())
        when(side, lambda: drain_raw(side))
    for h in range(heads):
        for side in sides_h:
            if h > 0:
                when(side, lambda: halo(qd, h, side, s_z, r_z).wait_send())
            when(side, lambda: back_q(h, side).wait_send())
        for side in sides_w:
            when(side, lambda: halo(kv, h, side, s_x, r_x).wait_send())
            when(side, lambda: back_kv(h, side).wait_send())

        for trip in range(2):
            for part, r in enumerate(ROUTES[trip][h]):
                if r == 0:
                    continue
                held = relay.at[trip, h, part]
                for _, via, _, _ in detours(r):
                    @pl.when(iw == via)
                    def _():
                        pltpu.make_async_copy(held, held, s_relay.at[trip, h, part]).wait()
    for h in range(heads):
        part = res.at[:, :, pl.ds(0, nd * HD)]
        pltpu.make_async_copy(part, part, r_out.at[h]).wait()


def solution(mesh):
    nh, nw, nd = mesh.shape["ha"], mesh.shape["wa"], mesh.shape["hd"]
    spec = P("ha", "wa", "hd", None)

    def per_device(q, k, v, o, g, n):
        tok, chan = q.shape[2], q.shape[3]
        heads = chan // HD // nd
        tile = tok * nd
        lead = q.shape

        def kernel(*refs):
            body(nh, nw, nd, heads, tok, *refs)

        dma = pltpu.SemaphoreType.DMA
        res = pl.pallas_call(
            kernel,
            out_shape=pltpu.VMEM((3, tok, chan), BF16),
            in_specs=[pl.BlockSpec(memory_space=pltpu.HBM)] * 6,
            out_specs=pl.BlockSpec(memory_space=pltpu.VMEM),
            scratch_shapes=[
                pltpu.VMEM((4, tok, chan), BF16),
                pltpu.VMEM((tok, chan), BF16),
                pltpu.VMEM((n.shape[3], tok), F32),
                pltpu.VMEM((64, 128), F32),
                pltpu.VMEM((3, heads, 2, tile, HD), BF16),
                pltpu.VMEM((3, heads, 2, tile, HD), BF16),
                pltpu.VMEM((128, 128), F32),
                pltpu.VMEM((64, 128), F32),
                pltpu.VMEM((nd, 8, 128), F32),
                pltpu.VMEM((3, 8, tile), F32),
                pltpu.VMEM((3, HD, tile), BF16),
                pltpu.VMEM((heads, 3, HD, tile), F32),
                pltpu.VMEM((heads, 3, 2, tile, HD), F32),
                pltpu.VMEM((2, heads, HD, tile), BF16),
                pltpu.VMEM((2, heads, HD, tile), BF16),
                pltpu.VMEM((2, heads, 2, tile, HD), BF16),
                pltpu.VMEM((2, heads, 2, tile, HD), BF16),
                pltpu.VMEM((heads, 3, tile, HD), BF16),
                pltpu.VMEM((2, heads, 2, tile, HD), BF16),
                pltpu.VMEM((2, 2, tok, nd * HD), BF16),
                dma((6,)),
                dma((heads, 2, nd - 1)), dma((heads, 2)),
                dma((nd - 1,)), dma((1,)),
                dma((heads, 2)), dma((heads, 2)),
                dma((heads, 2)), dma((heads, 2)),
                dma((2,)), dma((2,)),
                dma((2, heads)), dma((2, heads)),
                dma((2, heads)), dma((2, heads)),
                dma((heads, nd - 1)), dma((heads, nd - 1)), dma((heads,)),
                dma((2, heads, 2)), dma((2, heads, 2)),
                dma((2,)), dma((2,)), dma((2, nd - 1)),
            ],
            compiler_params=pltpu.CompilerParams(
                collective_id=0, has_side_effects=True, vmem_limit_bytes=60 * 1024 * 1024
            ),
        )(*(x.reshape(x.shape[2:]) for x in (q, k, v, o, g)), n.reshape(n.shape[2:]).T)
        return tuple(res[i].reshape(lead) for i in range(3))

    return jax.shard_map(
        per_device, mesh=mesh, in_specs=(spec,) * 6, out_specs=(spec,) * 3, check_vma=False
    )
```

```python
import jax
import jax.numpy as jnp
from jax import lax
from jax.experimental import pallas as pl
from jax.experimental.pallas import tpu as pltpu
from jax.sharding import PartitionSpec as P

HD = 128
ROUTES = (((0, 1), (0, 1), (0, 1)), ((2, 3), (0, 1), (0, 0)))
MESH = pl.DeviceIdType.MESH
F32 = jnp.float32
BF16 = jnp.bfloat16
NT = (((1,), (1,)), ((), ()))
NN = (((1,), (0,)), ((), ()))


def dot(a, b, dims):
    return lax.dot_general(a, b, dims, preferred_element_type=F32)


def body(
    nh, nw, nd, heads, tok,
    q_hbm, k_hbm, v_hbm, o_hbm, g_hbm, n_hbm,
    res,
    xin, o_in, n_in, n_out, qd, kv, pad, st_out, st_in, st,
    k_t, dq_acc, kv_acc, rq_send, rq_recv, rk_send, rk_recv, out_send, relay, raw,
    sem_load, s_in, r_in, s_st, r_st, s_z, r_z, s_x, r_x, s_sz, r_sz,
    s_rq, r_rq, s_rk, r_rk, s_out, s_out2, r_out, s_relay, r_relay, s_raw, r_raw, s_spread,
):
    ih, iw, me = lax.axis_index("ha"), lax.axis_index("wa"), lax.axis_index("hd")
    tile = nd * tok
    scale = HD ** -0.5
    sides_h = (("ha", ih > 0, ih - 1, 0, 2), ("ha", ih < nh - 1, ih + 1, 2, 0))
    sides_w = (("wa", iw > 0, iw - 1, 0, 2), ("wa", iw < nw - 1, iw + 1, 2, 0))
    mid = nw // 2
    vias = (0, 1, 2)
    at_mid = (iw == mid - 1) | (iw == mid)
    detours = lambda r: ((mid - 1, vias[r - 1], mid, 0), (mid, nw - 1 - vias[r - 1], mid - 1, 2))
    met = [(m, v) for m in (mid - 1, mid) for w in vias for v in (w, nw - 1 - w) if abs(m - v) > 1]

    barrier = pltpu.get_barrier_semaphore()

    def greet(t, c):
        pl.semaphore_signal(barrier, inc=1, device_id={"hd": lax.rem(me + 1 + t, nd)}, device_id_type=MESH)
        return c

    lax.fori_loop(0, nd - 1, greet, 0)
    for axis, exists, other, _, _ in sides_h + sides_w:
        @pl.when(exists)
        def _():
            pl.semaphore_signal(barrier, inc=1, device_id={axis: other}, device_id_type=MESH)
    for m, v in met:
        for here, other in ((m, v), (v, m)):
            @pl.when(iw == here)
            def _():
                pl.semaphore_signal(barrier, inc=1, device_id={"wa": other}, device_id_type=MESH)

    loads = [
        pltpu.make_async_copy(src, dst, sem_load.at[n])
        for n, (src, dst) in enumerate((
            (q_hbm, xin.at[0]), (g_hbm, xin.at[1]), (k_hbm, xin.at[2]), (v_hbm, xin.at[3]),
            (o_hbm, o_in), (n_hbm, n_in),
        ))
    ]
    for load in loads:
        load.start()

    for _, exists, _, slot, _ in sides_h:
        @pl.when(jnp.logical_not(exists))
        def _():
            qd[slot] = jnp.zeros(qd.shape[1:], BF16)
            st[slot] = jnp.zeros(st.shape[1:], F32)
            rq_recv[slot // 2] = jnp.zeros(rq_recv.shape[1:], BF16)
    for _, exists, _, slot, _ in sides_w:
        @pl.when(jnp.logical_not(exists))
        def _():
            kv[slot] = jnp.zeros(kv.shape[1:], BF16)
            rk_recv[slot // 2] = jnp.zeros(rk_recv.shape[1:], BF16)

    for load in loads[:4]:
        load.wait()
    count = jnp.int32(nd - 1)
    for _, exists, _, _, _ in sides_h + sides_w:
        count = count + exists.astype(jnp.int32)
    for m, v in met:
        count = count + ((iw == m) | (iw == v)).astype(jnp.int32)
    pl.semaphore_wait(barrier, count)

    def when(side, fn):
        @pl.when(side[1])
        def _():
            fn()

    my_rows = pl.ds(pl.multiple_of(me * tok, tok), tok)

    def spread(h, part, dst):
        def lanes(d):
            return pl.ds(pl.multiple_of((h * nd + d) * HD, HD), HD)

        def one(t, c):
            d = lax.rem(me + 1 + t, nd)
            pltpu.make_async_remote_copy(
                src_ref=xin.at[pl.ds(2 * part, 2), :, lanes(d)],
                dst_ref=dst.at[1, h, :, my_rows, :],
                send_sem=s_in.at[h, part, t], recv_sem=r_in.at[h, part],
                device_id={"hd": d}, device_id_type=MESH,
            ).start()
            return c

        lax.fori_loop(0, nd - 1, one, 0)
        pltpu.make_async_copy(
            xin.at[pl.ds(2 * part, 2), :, lanes(me)], dst.at[1, h, :, my_rows, :], r_in.at[h, part]
        ).start()

    def raw_halo(side):
        axis, _, other, slot, there = side
        return pltpu.make_async_remote_copy(
            src_ref=xin.at[pl.ds(0, 2), :, pl.ds(0, nd * HD)], dst_ref=raw.at[there // 2],
            send_sem=s_raw.at[slot // 2], recv_sem=r_raw.at[there // 2],
            device_id={axis: other}, device_id_type=MESH,
        )

    for side in sides_h:
        when(side, lambda: raw_halo(side).start())
    spread(0, 1, kv)
    spread(1, 0, qd)
    spread(0, 0, qd)

    for load in loads[4:]:
        load.wait()
    lane = lax.broadcasted_iota(jnp.int32, (tok, 128), 1)
    table = jnp.zeros((tok, 128), F32)
    n_out[...] = jnp.zeros(n_out.shape, F32)
    for g in range(nd * heads):
        h, d = g // nd, g % nd
        cols = slice(g * HD, (g + 1) * HD)
        dots = jnp.sum(xin[1, :, cols].astype(F32) * o_in[:, cols].astype(F32), axis=1, keepdims=True)
        n_out[8 * d + h:8 * d + h + 1, :tok] = n_in[g:g + 1, :]
        table = jnp.where(lane == 8 * d + heads + h, dots, table)
    pad[...] = jnp.zeros(pad.shape, F32)
    pad[pl.ds(pl.multiple_of(lax.rem(me, 4) * tok, tok), tok), :] = table
    st_out[...] = pad[...].T[:64] + pltpu.roll(n_out[...], lax.rem(me, 4) * tok, 1)

    def spread_stats(t, c):
        d = lax.rem(me + 1 + t, nd)
        pltpu.make_async_remote_copy(
            src_ref=st_out.at[pl.ds(pl.multiple_of(d * 8, 8), 8), :], dst_ref=st_in.at[me],
            send_sem=s_st.at[t], recv_sem=r_st.at[0], device_id={"hd": d}, device_id_type=MESH,
        ).start()
        return c

    lax.fori_loop(0, nd - 1, spread_stats, 0)
    pltpu.make_async_copy(
        st_out.at[pl.ds(pl.multiple_of(me * 8, 8), 8), :], st_in.at[me], r_st.at[0]
    ).start()

    def halo(buf, h, side, send, recv):
        axis, _, other, slot, there = side
        return pltpu.make_async_remote_copy(
            src_ref=buf.at[1, h], dst_ref=buf.at[there, h],
            send_sem=send.at[h, slot // 2], recv_sem=recv.at[h, there // 2],
            device_id={axis: other}, device_id_type=MESH,
        )

    def seam(side):
        return at_mid & (side[2] == (2 * mid - 1) - iw)

    def leg(src, dst, send, recv, to):
        return pltpu.make_async_remote_copy(
            src_ref=src, dst_ref=dst, send_sem=send, recv_sem=recv,
            device_id={"wa": to}, device_id_type=MESH,
        )

    def send_kv(h, side, src, dst, send, recv, trip):
        @pl.when(side[1] & jnp.logical_not(seam(side)))
        def _():
            leg(src, dst, send, recv, side[2]).start()

        @pl.when(side[1] & seam(side))
        def _():
            for n in range(heads):
                @pl.when(h == n)
                def _():
                    for part, r in enumerate(ROUTES[trip][n]):
                        if r == 0:
                            leg(src.at[part], dst.at[part], send, recv, side[2]).start()
                        else:
                            up, down = detours(r)
                            leg(
                                src.at[part], relay.at[trip, n, part], send, r_relay.at[trip, n, part],
                                jnp.where(iw == mid - 1, up[1], down[1]),
                            ).start()

    def pass_on(h, buf_of, sem_of, trip):
        for part, r in enumerate(ROUTES[trip][h]):
            if r == 0:
                continue
            held = relay.at[trip, h, part]
            for _, via, target, there in detours(r):
                @pl.when(iw == via)
                def _():
                    pltpu.make_async_copy(held, held, r_relay.at[trip, h, part]).wait()
                    leg(held, buf_of(there).at[part], s_relay.at[trip, h, part], sem_of(there), target).start()

    def pass_kv(h):
        pass_on(h, lambda there: kv.at[there, h], lambda there: r_x.at[h, there // 2], 0)

    def pass_back(h):
        pass_on(h, lambda there: rk_recv.at[there // 2, h], lambda there: r_rk.at[there // 2, h], 1)

    def halo_stats(side):
        axis, _, other, slot, there = side
        return pltpu.make_async_remote_copy(
            src_ref=st.at[1], dst_ref=st.at[there],
            send_sem=s_sz.at[slot // 2], recv_sem=r_sz.at[there // 2],
            device_id={axis: other}, device_id_type=MESH,
        )

    def spread_raw(side):
        n = side[3] // 2
        pltpu.make_async_copy(raw.at[n], raw.at[n], r_raw.at[n]).wait()

        def one(t, c):
            d = lax.rem(me + 1 + t, nd)
            pltpu.make_async_remote_copy(
                src_ref=raw.at[n, :, :, pl.ds(pl.multiple_of(d * HD, HD), HD)],
                dst_ref=qd.at[side[3], 0, :, my_rows, :],
                send_sem=s_spread.at[n, t], recv_sem=r_z.at[0, n],
                device_id={"hd": d}, device_id_type=MESH,
            ).start()
            return c

        lax.fori_loop(0, nd - 1, one, 0)
        pltpu.make_async_copy(
            raw.at[n, :, :, pl.ds(pl.multiple_of(me * HD, HD), HD)],
            qd.at[side[3], 0, :, my_rows, :], r_z.at[0, n],
        ).start()

    def own(buf, h, part):
        pltpu.make_async_copy(buf.at[1, h], buf.at[1, h], r_in.at[h, part]).wait()

    def send_rows(h):
        own(qd, h, 0)
        for side in sides_h:
            when(side, lambda: halo(qd, h, side, s_z, r_z).start())

    def send_columns(h):
        own(kv, h, 1)
        for side in sides_w:
            send_kv(h, side, kv.at[1, h], kv.at[side[4], h], s_x.at[h, side[3] // 2], r_x.at[h, side[4] // 2], 0)

    send_columns(0)
    send_rows(1)
    spread(1, 1, kv)
    spread(2, 0, qd)
    pltpu.make_async_copy(st_in, st_in, r_st.at[0]).wait()
    got = st_in[...]
    st[1] = jnp.concatenate(
        [got[0] + got[1] + got[2] + got[3], got[4] + got[5] + got[6] + got[7]], axis=1
    )
    for side in sides_h:
        when(side, lambda: halo_stats(side).start())
    own(qd, 0, 0)
    for side in sides_h:
        when(side, lambda: spread_raw(side))
    spread(2, 1, kv)
    pass_kv(0)
    send_columns(1)
    send_rows(2)
    pass_kv(1)
    send_columns(2)
    pass_kv(2)

    def arrived(buf, slot, h, sem):
        pltpu.make_async_copy(buf.at[slot, h], buf.at[slot, h], sem.at[h, slot // 2]).wait()

    def back_q(h, side):
        axis, _, other, slot, there = side
        return pltpu.make_async_remote_copy(
            src_ref=rq_send.at[slot // 2, h], dst_ref=rq_recv.at[there // 2, h],
            send_sem=s_rq.at[slot // 2, h], recv_sem=r_rq.at[there // 2, h],
            device_id={axis: other}, device_id_type=MESH,
        )

    def back_kv(h, side):
        axis, _, other, slot, there = side
        return pltpu.make_async_remote_copy(
            src_ref=rk_send.at[slot // 2, h], dst_ref=rk_recv.at[there // 2, h],
            send_sem=s_rk.at[slot // 2, h], recv_sem=r_rk.at[there // 2, h],
            device_id={axis: other}, device_id_type=MESH,
        )

    first_b = jnp.where(iw == mid, 2, 0)
    last_b = 2 - first_b

    def wait_columns(h, b):
        for side in sides_w:
            @pl.when(side[1] & (b == side[3]))
            def _():
                arrived(kv, side[3], h, r_x)

    def compute(h):
        def pair(a, b, new_q, new_kv):
            q, g = qd[a, h, 0], qd[a, h, 1]
            norm = st[a, pl.ds(h, 1), :]
            dots = st[a, pl.ds(heads + h, 1), :]
            s_t = dot(kv[b, h, 0], q, NT)
            p_t = jnp.exp(s_t * scale - norm)
            dp_t = dot(kv[b, h, 1], g, NT)
            ds_t = (p_t * (dp_t - dots) * scale).astype(BF16)
            dk = dot(ds_t, q, NN)
            dv = dot(p_t.astype(BF16), g, NN)
            dq = dot(k_t[b], ds_t, NN)
            if new_q:
                dq_acc[h, a] = dq
            else:
                dq_acc[h, a] += dq
            if new_kv:
                kv_acc[h, b, 0] = dk
                kv_acc[h, b, 1] = dv
            else:
                kv_acc[h, b, 0] += dk
                kv_acc[h, b, 1] += dv

        def back_columns(b):
            for side in sides_w:
                slot = side[3]

                @pl.when(b == slot)
                def _():
                    rk_send[slot // 2, h] = kv_acc[h, slot].astype(BF16)
                    send_kv(
                        h, side, rk_send.at[slot // 2, h], rk_recv.at[side[4] // 2, h],
                        s_rk.at[slot // 2, h], r_rk.at[side[4] // 2, h], 1,
                    )

        def back_rows(a):
            rq_send[a // 2, h] = dq_acc[h, a].astype(BF16)
            when(sides_h[a // 2], lambda: back_q(h, sides_h[a // 2]).start())

        k_t[1] = kv[1, h, 0].T
        pair(1, 1, True, True)
        wait_columns(h, first_b)
        k_t[first_b] = kv[first_b, h, 0].T
        pair(1, first_b, False, True)
        for side in sides_h:
            when(side, lambda: arrived(qd, side[3], h, r_z))

            @pl.when(side[1] & (h == 0))
            def _():
                pltpu.make_async_copy(st.at[side[3]], st.at[side[3]], r_sz.at[side[3] // 2]).wait()
        pair(0, first_b, True, False)
        pair(2, first_b, True, False)
        back_columns(first_b)
        pair(0, 1, False, False)
        pair(2, 1, False, False)
        wait_columns(h, last_b)
        k_t[last_b] = kv[last_b, h, 0].T
        pair(0, last_b, False, True)
        back_rows(0)
        pair(2, last_b, False, False)
        back_rows(2)
        pair(1, last_b, False, False)
        back_columns(last_b)

    def out_copy(h, t, rows, sem):
        d = lax.rem(me + 1 + t, nd)
        return pltpu.make_async_remote_copy(
            src_ref=out_send.at[h, rows, pl.ds(pl.multiple_of(d * tok, tok), tok), :],
            dst_ref=res.at[rows, :, pl.ds(pl.multiple_of((h * nd + me) * HD, HD), HD)],
            send_sem=sem.at[h, t], recv_sem=r_out.at[h],
            device_id={"hd": d}, device_id_type=MESH,
        )

    def send_out(h, rows, sem):
        def one(t, c):
            out_copy(h, t, rows, sem).start()
            return c

        lax.fori_loop(0, nd - 1, one, 0)
        pltpu.make_async_copy(
            out_send.at[h, rows, my_rows, :],
            res.at[rows, :, pl.ds(pl.multiple_of((h * nd + me) * HD, HD), HD)],
            r_out.at[h],
        ).start()

    def finish(h):
        for n, side in enumerate(sides_h):
            when(side, lambda: pltpu.make_async_copy(
                rq_recv.at[n, h], rq_recv.at[n, h], r_rq.at[n, h]).wait())
        dq = dq_acc[h, 1] + rq_recv[0, h].astype(F32) + rq_recv[1, h].astype(F32)
        out_send[h, 0] = dq.T.astype(BF16)
        send_out(h, pl.ds(0, 1), s_out)
        for n, side in enumerate(sides_w):
            when(side, lambda: pltpu.make_async_copy(
                rk_recv.at[n, h], rk_recv.at[n, h], r_rk.at[n, h]).wait())
        for n in range(2):
            out_send[h, 1 + n] = (
                kv_acc[h, 1, n] + rk_recv[0, h, n].astype(F32) + rk_recv[1, h, n].astype(F32)
            ).astype(BF16)
        send_out(h, pl.ds(1, 2), s_out2)

    def step(h, c):
        compute(h)
        return c

    lax.fori_loop(0, heads, step, 0)
    for h in range(heads - 1):
        pass_back(h)

    def close(h, c):
        finish(h)

        @pl.when(h == 0)
        def _():
            pass_back(heads - 1)
        return c

    lax.fori_loop(0, heads, close, 0)

    def drain(t, c):
        d = lax.rem(me + 1 + t, nd)
        for h in range(heads):
            for part in range(2):
                src = xin.at[pl.ds(2 * part, 2), :, pl.ds(0, HD)]
                pltpu.make_async_copy(src, src, s_in.at[h, part, t]).wait()
            for rows, sem in ((pl.ds(0, 1), s_out), (pl.ds(1, 2), s_out2)):
                src = out_send.at[h, rows, pl.ds(0, tok), :]
                pltpu.make_async_copy(src, src, sem.at[h, t]).wait()
        src = st_out.at[pl.ds(0, 8), :]
        pltpu.make_async_copy(src, src, s_st.at[t]).wait()
        return c

    lax.fori_loop(0, nd - 1, drain, 0)
    def drain_raw(side):
        def one(t, c):
            src = raw.at[side[3] // 2, :, :, pl.ds(0, HD)]
            pltpu.make_async_copy(src, src, s_spread.at[side[3] // 2, t]).wait()
            return c

        raw_halo(side).wait_send()
        lax.fori_loop(0, nd - 1, one, 0)

    for side in sides_h:
        when(side, lambda: halo_stats(side).wait_send())
        when(side, lambda: drain_raw(side))
    for h in range(heads):
        for side in sides_h:
            if h > 0:
                when(side, lambda: halo(qd, h, side, s_z, r_z).wait_send())
            when(side, lambda: back_q(h, side).wait_send())
        for side in sides_w:
            when(side, lambda: halo(kv, h, side, s_x, r_x).wait_send())
            when(side, lambda: back_kv(h, side).wait_send())

        for trip in range(2):
            for part, r in enumerate(ROUTES[trip][h]):
                if r == 0:
                    continue
                held = relay.at[trip, h, part]
                for _, via, _, _ in detours(r):
                    @pl.when(iw == via)
                    def _():
                        pltpu.make_async_copy(held, held, s_relay.at[trip, h, part]).wait()
    for h in range(heads):
        part = res.at[:, :, pl.ds(0, nd * HD)]
        pltpu.make_async_copy(part, part, r_out.at[h]).wait()


def solution(mesh):
    nh, nw, nd = mesh.shape["ha"], mesh.shape["wa"], mesh.shape["hd"]
    spec = P("ha", "wa", "hd", None)

    def per_device(q, k, v, o, g, n):
        tok, chan = q.shape[2], q.shape[3]
        heads = chan // HD // nd
        tile = tok * nd
        lead = q.shape

        def kernel(*refs):
            body(nh, nw, nd, heads, tok, *refs)

        dma = pltpu.SemaphoreType.DMA
        res = pl.pallas_call(
            kernel,
            out_shape=pltpu.VMEM((3, tok, chan), BF16),
            in_specs=[pl.BlockSpec(memory_space=pltpu.HBM)] * 6,
            out_specs=pl.BlockSpec(memory_space=pltpu.VMEM),
            scratch_shapes=[
                pltpu.VMEM((4, tok, chan), BF16),
                pltpu.VMEM((tok, chan), BF16),
                pltpu.VMEM((n.shape[3], tok), F32),
                pltpu.VMEM((64, 128), F32),
                pltpu.VMEM((3, heads, 2, tile, HD), BF16),
                pltpu.VMEM((3, heads, 2, tile, HD), BF16),
                pltpu.VMEM((128, 128), F32),
                pltpu.VMEM((64, 128), F32),
                pltpu.VMEM((nd, 8, 128), F32),
                pltpu.VMEM((3, 8, tile), F32),
                pltpu.VMEM((3, HD, tile), BF16),
                pltpu.VMEM((heads, 3, HD, tile), F32),
                pltpu.VMEM((heads, 3, 2, tile, HD), F32),
                pltpu.VMEM((2, heads, HD, tile), BF16),
                pltpu.VMEM((2, heads, HD, tile), BF16),
                pltpu.VMEM((2, heads, 2, tile, HD), BF16),
                pltpu.VMEM((2, heads, 2, tile, HD), BF16),
                pltpu.VMEM((heads, 3, tile, HD), BF16),
                pltpu.VMEM((2, heads, 2, tile, HD), BF16),
                pltpu.VMEM((2, 2, tok, nd * HD), BF16),
                dma((6,)),
                dma((heads, 2, nd - 1)), dma((heads, 2)),
                dma((nd - 1,)), dma((1,)),
                dma((heads, 2)), dma((heads, 2)),
                dma((heads, 2)), dma((heads, 2)),
                dma((2,)), dma((2,)),
                dma((2, heads)), dma((2, heads)),
                dma((2, heads)), dma((2, heads)),
                dma((heads, nd - 1)), dma((heads, nd - 1)), dma((heads,)),
                dma((2, heads, 2)), dma((2, heads, 2)),
                dma((2,)), dma((2,)), dma((2, nd - 1)),
            ],
            compiler_params=pltpu.CompilerParams(
                collective_id=0, has_side_effects=True, vmem_limit_bytes=60 * 1024 * 1024
            ),
        )(*(x.reshape(x.shape[2:]) for x in (q, k, v, o, g)), n.reshape(n.shape[2:]).T)
        return tuple(res[i].reshape(lead) for i in range(3))

    return jax.shard_map(
        per_device, mesh=mesh, in_specs=(spec,) * 6, out_specs=(spec,) * 3, check_vma=False
    )
```
